512 devices in a mesh: lat: 16 (over z_hi, x), lon: 32 (over z_lo, y, core).
Axes of the slice: x: 4, y: 8, z: 8 (z_hi: 4, z_lo: 2; z = z_hi * 2 + z_lo), core: 2. Of those that a mesh axis runs over, the one named last changes fastest.
Arguments:
- state_grid: bfloat16 [1, 384, 768, 256], P(None, 'lat', 'lon'), may hold values from -6 to 6
- spectral_filter: float32 [384, 256], P(None, 'lon'), may hold values from -6 to 6
- up_weight: bfloat16 [256, 512], replicated, may hold values from -0.375 to 0.375
- down_weight: bfloat16 [256, 512], replicated, may hold values from -0.25 to 0.25
- cotangent: bfloat16 [1, 384, 768, 256], P(None, 'lat', 'lon'), may hold values from -6 to 6
Outputs:
- grad_field: bfloat16 [1, 384, 768, 256], P(None, 'lat', 'lon')
- grad_up: float32 [256, 512], P('lat')
- grad_down: float32 [256, 512], P('lat')
The draws below stay inside these ranges and needn't reach their ends.
All inputs are finite; a program needn't handle non-finite values.
Results may differ from the reference program's by a relative error of at most 0.018.
Values may be sent and summed in bfloat16 or wider, within the bound.
No kernel may reach another device: no remote copies, remote signals or barrier semaphores. Data moves between devices by JAX's collectives and lax.ppermute only.
A program may use at most 64 MiB of HBM per device.

```python
import math
import jax
import jax.numpy as jnp
from jax import lax

NLAT = 384
NLON = 768
L = 384
C = 256
H = 512
B = 1


def level_of(stream_key, shape, split, low, high):
    def one(position, shards_of):
        steps = jax.random.uniform(jax.random.fold_in(jax.random.fold_in(stream_key, 6), position), (shards_of,), jnp.float32, low / len(split), high / len(split))
        return jnp.repeat(jnp.exp(steps), shape[position] // shards_of).reshape((-1,) + (1,) * (len(shape) - position - 1))

    loudness = one(*split[0])
    for cut in split[1:]:
        loudness = loudness * one(*cut)
    return loudness


def noise(stream_key, extent, scale, reach, split=(), held_as=jnp.bfloat16):
    loudness = level_of(stream_key, extent, split, -0.22, 0.18) if split else 1.0
    entries = jax.random.normal(stream_key, extent, jnp.float32) * scale * loudness
    return jnp.minimum(jnp.maximum(entries, -reach), reach).astype(held_as)


def setup_inputs(seed: int = 0) -> dict:
    seeds = jax.random.split(jax.random.key(seed), 6)
    return {
        "state_grid": noise(seeds[0], (B, NLAT, NLON, C), 1.0, 6.0, ((1, 16), (2, 32))),
        "spectral_filter": noise(seeds[1], (L, C), 1.0, 6.0, ((1, 32),), jnp.float32),
        "up_weight": noise(seeds[2], (C, H), C ** -0.5, 0.375),
        "down_weight": noise(seeds[3], (C, H), H ** -0.5, 0.25),
        "cotangent": noise(seeds[4], (B, NLAT, NLON, C), 1.0, 6.0, ((1, 16), (2, 32))),
    }


def fourier_tables(lon_total, order_total):
    lon_index = jnp.arange(lon_total, dtype=jnp.int32)
    order_index = jnp.arange(order_total, dtype=jnp.int32)
    phases = lon_index[:, None] * order_index[None, :] % lon_total
    angles = phases.astype(jnp.float32) * (2.0 * math.pi / lon_total)
    cosine = jnp.cos(angles)
    sines = jnp.sin(angles)
    forward = jnp.concatenate([cosine, -sines], axis=1).astype(jnp.bfloat16)
    doubling = jnp.where(order_index == 0, 1.0, 2.0).astype(jnp.float32)
    inverse = jnp.concatenate([(cosine * doubling[None, :]).T, (-sines * doubling[None, :]).T], axis=0).astype(jnp.bfloat16)
    return (forward, inverse)

def row_scale(lat_total, lon_total):
    colatitude = (jnp.arange(lat_total, dtype=jnp.float32) + 0.5) * (math.pi / lat_total)
    counter = jnp.arange(1, lat_total // 2 + 1, dtype=jnp.float32)
    series = lax.optimization_barrier(jnp.sum(jnp.cos(2.0 * counter[None, :] * colatitude[:, None]) / (4.0 * counter * counter - 1.0)[None, :], axis=1))
    return 2.0 / lat_total * (1.0 - 2.0 * series) * (2.0 * math.pi / lon_total)

def combine_transfer(early, late):
    e00, e01, e10, e11, early_log = early
    l00, l01, l10, l11, late_log = late
    p00 = l00 * e00 + l01 * e10
    p01 = l00 * e01 + l01 * e11
    p10 = l10 * e00 + l11 * e10
    p11 = l10 * e01 + l11 * e11
    largest = jnp.maximum(jnp.maximum(jnp.abs(p00), jnp.abs(p01)), jnp.maximum(jnp.abs(p10), jnp.abs(p11)))
    return (p00 / largest, p01 / largest, p10 / largest, p11 / largest, early_log + late_log + jnp.log(largest))

def legendre_table(order_first, order_count, lat_total, degrees):
    half_rows = lat_total // 2
    colatitude = (jnp.arange(half_rows, dtype=jnp.float32) + 0.5) * (math.pi / lat_total)
    cosine = jnp.cos(colatitude)
    log_sine = jnp.log(jnp.sin(colatitude))
    later = jnp.arange(1, degrees, dtype=jnp.float32)
    ratios = jnp.log((2.0 * later - 1.0) / (2.0 * later))
    every_order = jnp.arange(degrees, dtype=jnp.float32)
    partial_logs = lax.optimization_barrier(jnp.sum(jnp.where(later[None, :] <= every_order[:, None], ratios[None, :], 0.0), axis=1))
    base_logs = 0.5 * (jnp.log((2.0 * every_order + 1.0) / (4.0 * math.pi)) + partial_logs)
    base_logs = lax.dynamic_slice_in_dim(base_logs, order_first, order_count)
    orders = (order_first + jnp.arange(order_count, dtype=jnp.int32)).astype(jnp.float32)[:, None]
    diag_logs = base_logs[:, None] + orders * log_sine[None, :]
    squares = orders * orders
    full_shape = (order_count, half_rows)
    block_len = 16

    def one_block(carry, block_index):
        outputs = []
        for inner in range(block_len):
            degree_val = (block_index * block_len + inner).astype(jnp.float32)
            spread = jnp.maximum(degree_val * degree_val - squares, 1.0)
            growth = jnp.sqrt(jnp.maximum(4.0 * degree_val * degree_val - 1.0, 1.0) / spread)
            lower_deg = degree_val - 1.0
            damping = jnp.sqrt(jnp.maximum(lower_deg * lower_deg - squares, 0.0) / jnp.maximum(4.0 * lower_deg * lower_deg - 1.0, 1.0))
            live = jnp.broadcast_to(degree_val > orders, full_shape)
            top_left = jnp.where(live, growth * cosine[None, :], 1.0)
            top_right = jnp.where(live, jnp.broadcast_to(-growth * damping, full_shape), 0.0)
            bottom_left = jnp.where(live, 1.0, 0.0).astype(jnp.float32)
            bottom_right = jnp.where(live, 0.0, 1.0).astype(jnp.float32)
            log_zero = jnp.zeros(full_shape, jnp.float32)
            carry = combine_transfer(carry, (top_left, top_right, bottom_left, bottom_right, log_zero))
            values = jnp.exp(diag_logs + carry[4]) * carry[0]
            values = jnp.where(degree_val >= orders, values, 0.0)
            outputs.append(values.astype(jnp.bfloat16))
        return (carry, jnp.stack(outputs))
    ones_init = jnp.ones(full_shape, jnp.float32)
    zeros_init = jnp.zeros(full_shape, jnp.float32)
    start_carry = (ones_init, zeros_init, zeros_init, ones_init, zeros_init)
    _, blocks = lax.scan(one_block, start_carry, jnp.arange(degrees // block_len, dtype=jnp.int32))
    return blocks.reshape(degrees, order_count, half_rows)

def parity_signs(order_first, order_count, degrees):
    degree_index = jnp.arange(degrees, dtype=jnp.int32)
    order_index = order_first + jnp.arange(order_count, dtype=jnp.int32)
    return (1 - 2 * ((degree_index[:, None] + order_index[None, :]) % 2)).astype(jnp.float32)

def analysis(fourier_modes, legendre, parity):
    half_rows = legendre.shape[2]
    table_wide = legendre.astype(jnp.float32)
    northern = fourier_modes[:, :half_rows].astype(jnp.float32)
    southern = jnp.flip(fourier_modes[:, half_rows:], axis=1).astype(jnp.float32)
    north_sum = jnp.einsum('lmk,bkcpm->bcplm', table_wide, northern)
    south_sum = jnp.einsum('lmk,bkcpm->bcplm', table_wide, southern)
    return north_sum + parity * south_sum

def synthesis(coefs, legendre, parity_low):
    table_wide = legendre.astype(jnp.float32)
    north_sum = jnp.einsum('lmk,bcplm->bkcpm', table_wide, coefs.astype(jnp.float32))
    mirrored = (coefs * parity_low).astype(jnp.float32)
    south_sum = jnp.einsum('lmk,bcplm->bkcpm', table_wide, mirrored)
    return jnp.concatenate([north_sum, jnp.flip(south_sum, axis=1)], axis=1)

def gelu_slope(values):
    normal_cdf = 0.5 * (1.0 + lax.erf(values / math.sqrt(2.0)))
    return normal_cdf + values * jnp.exp(-0.5 * values * values) / math.sqrt(2.0 * math.pi)

def reference(state_grid, spectral_filter, up_weight, down_weight, cotangent):
    members = state_grid.shape[0]
    forward_table, inverse_table = fourier_tables(NLON, L)
    row_weights = row_scale(NLAT, NLON)
    legendre = legendre_table(0, L, NLAT, L)
    parity = parity_signs(0, L, L)
    parity_low = parity.astype(jnp.bfloat16)
    filter_gains = spectral_filter.T[None, :, None, :, None]

    def to_spectral(grid_vals, fourier_table, einsum_form, weights_rows):
        fourier_modes = jnp.einsum(einsum_form, grid_vals.astype(jnp.float32), fourier_table.astype(jnp.float32))
        if weights_rows is not None:
            fourier_modes = fourier_modes * weights_rows[None, :, None, None]
        fourier_modes = fourier_modes.astype(jnp.bfloat16).reshape(members, NLAT, C, 2, L)
        return analysis(fourier_modes, legendre, parity)

    def to_grid(coefs, fourier_table, einsum_form, weights_rows):
        wave_rows = synthesis(coefs, legendre, parity_low).astype(jnp.bfloat16)
        flat_waves = wave_rows.reshape(members, NLAT, C, 2 * L)
        grid_vals = jnp.einsum(einsum_form, flat_waves.astype(jnp.float32), fourier_table.astype(jnp.float32))
        if weights_rows is not None:
            grid_vals = grid_vals * weights_rows[None, :, None, None]
        return grid_vals.astype(jnp.bfloat16)
    spectrum = to_spectral(state_grid, forward_table, 'bkjc,jn->bkcn', row_weights)
    filtered = (spectrum * filter_gains).astype(jnp.bfloat16)
    smooth = to_grid(filtered, inverse_table, 'bkcn,nj->bkjc', None)
    mixed_grid = (state_grid.astype(jnp.float32) + smooth.astype(jnp.float32)).astype(jnp.bfloat16)
    flat_mixed = mixed_grid.reshape(-1, C)
    pre_active = jnp.dot(flat_mixed, up_weight, preferred_element_type=jnp.float32)
    active = jax.nn.gelu(pre_active, approximate=False).astype(jnp.bfloat16)
    flat_cotangent = cotangent.reshape(-1, C)
    back_active = jnp.dot(flat_cotangent, down_weight, preferred_element_type=jnp.float32)
    back_pre = (back_active * gelu_slope(pre_active)).astype(jnp.bfloat16)
    back_mixed = flat_cotangent.astype(jnp.float32) + jnp.dot(back_pre, up_weight.T, preferred_element_type=jnp.float32)
    back_round = back_mixed.astype(jnp.bfloat16).reshape(state_grid.shape)
    back_spectrum = to_spectral(back_round, inverse_table, 'bkjc,nj->bkcn', None)
    back_filtered = (back_spectrum * filter_gains).astype(jnp.bfloat16)
    back_field = to_grid(back_filtered, forward_table, 'bkcn,jn->bkjc', row_weights)
    grad_field = (back_mixed.reshape(state_grid.shape) + back_field.astype(jnp.float32)).astype(jnp.bfloat16)
    grad_scale = 1.0 / math.sqrt(B * NLAT * NLON)
    grad_up = jnp.dot(flat_mixed.T, back_pre, preferred_element_type=jnp.float32) * grad_scale
    grad_down = jnp.dot(flat_cotangent.T, active, preferred_element_type=jnp.float32) * grad_scale
    return (grad_field, grad_up, grad_down)
```

```python
import functools
import math

import jax
import jax.numpy as jnp
from jax import lax
from jax.experimental import pallas as pl
from jax.experimental.pallas import tpu as pltpu
from jax.sharding import Mesh, PartitionSpec as P

L = 384
ROW_GROUPS = 4
TILE = 8
F32 = jnp.float32
BF16 = jnp.bfloat16
VMEM_LIMIT = 48 * 1024 * 1024


def dot(a, b, dims=((1,), (0,))):
    return lax.dot_general(a, b, (dims, ((), ())), preferred_element_type=F32)


def call(kernel, outs, *args, scratch=(), cost=None):
    single = not isinstance(outs, (list, tuple))
    shapes = [outs] if single else list(outs)
    result = pl.pallas_call(
        kernel,
        out_shape=shapes,
        in_specs=[pl.BlockSpec(memory_space=pltpu.VMEM)] * len(args),
        out_specs=[pl.BlockSpec(memory_space=pltpu.VMEM)] * len(shapes),
        scratch_shapes=list(scratch),
        compiler_params=pltpu.CompilerParams(vmem_limit_bytes=VMEM_LIMIT),
        cost_estimate=cost,
    )(*args)
    return result[0] if single else result


def shaped(shape, dtype):
    return jax.ShapeDtypeStruct(shape, dtype)


def tiles_of(rows, width):
    return pltpu.VMEM((-(-width // 128), rows, 128), F32)


def pick(ref, width, start=0, size=None, stride=1, lead=()):
    tiles = -(-width // 128)
    at = slice(None) if size is None else pl.ds(start, size, stride=stride)
    value = jnp.concatenate([ref[(*lead, i, at, slice(None))] for i in range(tiles)], axis=1)
    return value[:, :width] if tiles * 128 > width else value


def place(ref, value, start=0, size=None, stride=1, lead=()):
    pad = -value.shape[1] % 128
    if pad:
        value = jnp.concatenate([value, jnp.zeros((value.shape[0], pad), value.dtype)], axis=1)
    at = slice(None) if size is None else pl.ds(start, size, stride=stride)
    for i in range(value.shape[1] // 128):
        ref[(*lead, i, at, slice(None))] = value[:, i * 128 : (i + 1) * 128]


def row_scale(lat_total, lon_total):
    colatitude = (jnp.arange(lat_total, dtype=F32) + 0.5) * (math.pi / lat_total)
    counter = jnp.arange(1, lat_total // 2 + 1, dtype=F32)
    series = jnp.sum(
        jnp.cos(2.0 * counter[None, :] * colatitude[:, None])
        / (4.0 * counter * counter - 1.0)[None, :],
        axis=1,
    )
    return 2.0 / lat_total * (1.0 - 2.0 * series) * (2.0 * math.pi / lon_total)


def fourier_tables(lon_total, groups, per_group):
    row = jnp.arange(groups * TILE, dtype=jnp.int32)
    order = row // TILE * per_group + row % TILE
    live = row % TILE < per_group
    lon_index = jnp.arange(lon_total, dtype=jnp.int32)
    angles = (order[:, None] * lon_index[None, :] % lon_total).astype(F32) * (
        2.0 * math.pi / lon_total
    )
    tables = jnp.stack([jnp.cos(angles), -jnp.sin(angles)])
    tables = jnp.where(live[None, :, None], tables, 0.0).astype(BF16)
    return tables, jnp.swapaxes(tables, 1, 2)


def legendre_kernel(orders, degrees, m_ref, cos_ref, diag_ref, p_ref, pt_ref, table):
    m = m_ref[...]
    squares = m * m
    cosine = cos_ref[...]
    diag = diag_ref[...]

    def block(index, carry):
        here, before, scale = carry
        level = jnp.exp(diag + scale)
        for inner in range(TILE):
            degree = index * TILE + inner
            lv = jnp.full(m.shape, degree, jnp.int32).astype(F32)
            spread = jnp.maximum(lv * lv - squares, 1.0)
            growth = jnp.sqrt(jnp.maximum(4.0 * lv * lv - 1.0, 1.0) / spread)
            low = lv - 1.0
            damping = jnp.sqrt(
                jnp.maximum(low * low - squares, 0.0) / jnp.maximum(4.0 * low * low - 1.0, 1.0)
            )
            ahead = growth * cosine * here - growth * damping * before
            live = lv > m
            here, before = jnp.where(live, ahead, here), jnp.where(live, here, before)
            values = jnp.where(lv >= m, level * here, 0.0)
            place(table, values, pl.multiple_of(degree * TILE, TILE), TILE)
        largest = jnp.maximum(jnp.abs(here), jnp.abs(before))
        return here / largest, before / largest, scale + jnp.log(largest)

    ones = jnp.ones(m.shape, F32)
    zeros = jnp.zeros(m.shape, F32)
    lax.fori_loop(0, degrees // TILE, block, (ones, zeros, zeros))
    for r in range(orders):
        rows = pick(table, m.shape[1], r, degrees, TILE)
        p_ref[r] = rows.astype(BF16)
        pt_ref[r] = rows.T.astype(BF16)


def legendre_tables(first_order, orders, lat_total, groups, degrees):
    per = lat_total // groups
    half = lat_total // 2
    position = jnp.arange(lat_total, dtype=jnp.int32)
    row = position % groups * per + position // groups
    north = jnp.minimum(row, lat_total - 1 - row)
    colatitude = (north.astype(F32) + 0.5) * (math.pi / lat_total)
    cosine = jnp.where(row < half, 1.0, -1.0) * jnp.cos(colatitude)
    log_sine = jnp.log(jnp.sin(colatitude))
    later = jnp.arange(1, degrees, dtype=F32)
    ratios = jnp.log((2.0 * later - 1.0) / (2.0 * later))
    order = (first_order + jnp.arange(TILE, dtype=jnp.int32)).astype(F32)
    partial_logs = jnp.sum(jnp.where(later[None, :] <= order[:, None], ratios[None, :], 0.0), axis=1)
    base_logs = 0.5 * (jnp.log((2.0 * order + 1.0) / (4.0 * math.pi)) + partial_logs)
    shape = (TILE, lat_total)
    diag = base_logs[:, None] + order[:, None] * log_sine[None, :]
    return call(
        functools.partial(legendre_kernel, orders, degrees),
        [
            shaped((orders, degrees, lat_total), BF16),
            shaped((orders, lat_total, degrees), BF16),
        ],
        jnp.broadcast_to(order[:, None], shape),
        jnp.broadcast_to(cosine[None, :], shape),
        diag,
        scratch=[tiles_of(degrees * TILE, lat_total)],
        cost=pl.CostEstimate(flops=40_000_000, bytes_accessed=4_000_000, transcendentals=1_000_000),
    )


def put_tile(row_groups, load, store):
    first = load(0)
    cols, channels = first.shape
    store_row_groups, rows, chunk_count = row_groups
    channel_groups = chunk_count // store_row_groups
    wide = channels // channel_groups
    per = rows // store_row_groups
    pad = -(per * wide) % 128
    for q in range(store_row_groups):
        lines = [load(q * per + k).astype(F32) for k in range(per)]
        for g in range(channel_groups):
            parts = [line[:, g * wide : (g + 1) * wide] for line in lines]
            if pad:
                parts.append(jnp.zeros((cols, pad), F32))
            store(g * store_row_groups + q, jnp.concatenate(parts, axis=1).astype(BF16))


def take_row(row_groups, load_chunk, k):
    count, rows, chunk_count, wide = row_groups
    per = rows // count
    q, inner = k // per, k % per
    parts = [
        load_chunk(g * count + q)[:, inner * wide : (inner + 1) * wide].astype(F32)
        for g in range(chunk_count // count)
    ]
    return jnp.concatenate(parts, axis=1)


def split_kernel(row_groups, x_ref, out_ref):
    def store(chunk, value):
        out_ref[chunk] = value

    put_tile((row_groups, x_ref.shape[0], out_ref.shape[0]), lambda k: x_ref[k], store)


def forward_kernel(width, doubled, scaled, skip, *refs):
    if scaled:
        x_ref, table_ref, scale_ref, out_ref, x_all, out_all = refs
    else:
        x_ref, table_ref, out_ref, x_all, out_all = refs
    chunks, rows, _ = x_ref.shape
    cols = rows - skip
    for b in range(chunks):
        x_all[pl.ds(b * cols, cols), :] = x_ref[b, skip:, :].astype(F32)
    x = x_all[...].astype(BF16)
    halves = [dot(table_ref[p], x)[:, :width] for p in range(2)]
    value = jnp.concatenate(halves, axis=1)
    if scaled:
        value = value * scale_ref[...]
    if doubled:
        order_row = lax.broadcasted_iota(jnp.int32, value.shape, 0)
        value = value * jnp.where(order_row == 0, 1.0, 2.0)
    place(out_all, value)
    if skip:
        total = x_ref[0, :skip, :].astype(F32)
        for b in range(1, chunks):
            total = total + x_ref[b, :skip, :].astype(F32)
        bands = skip // 2
        lanes = total.shape[1]
        groups = value.shape[0] // TILE
        for q in range(groups // bands):
            for half in range(2):
                place(
                    out_all,
                    total[half * bands : (half + 1) * bands, :lanes],
                    q * TILE + TILE - 2 + half,
                    bands,
                    groups // bands * TILE,
                )
    out_ref[...] = pick(out_all, value.shape[1]).astype(BF16)


def spectral_kernel(orders, per, wide, x_ref, p_ref, pt_ref, gain_ref, out_ref, x_all, out_all):
    groups = x_ref.shape[0] // TILE
    place(x_all, x_ref[...].astype(F32))
    gains = jnp.concatenate([gain_ref[...], gain_ref[...]], axis=1)
    half = per * wide
    for r in range(orders):
        rows = pick(x_all, 2 * half, r, groups, TILE)
        modes = jnp.concatenate(
            [
                jnp.concatenate(
                    [rows[:, p * half + k * wide : p * half + (k + 1) * wide] for p in range(2)],
                    axis=1,
                )
                for k in range(per)
            ],
            axis=0,
        ).astype(BF16)
        spectrum = dot(p_ref[r], modes)
        filtered = (spectrum * gains).astype(BF16)
        waves = dot(pt_ref[r], filtered)
        parts = []
        for p in range(2):
            for k in range(per):
                parts.append(waves[k * groups : (k + 1) * groups, p * wide : (p + 1) * wide])
        place(out_all, jnp.concatenate(parts, axis=1), r, groups, TILE)
    for r in range(orders, TILE):
        place(out_all, jnp.zeros((groups, 2 * half), F32), r, groups, TILE)
    out_ref[...] = pick(out_all, 2 * half).astype(BF16)


def inverse_kernel(width, doubled, scaled, *refs):
    if scaled:
        x_ref, table_ref, scale_ref, out_ref = refs
    else:
        x_ref, table_ref, out_ref = refs
    x = x_ref[...]
    if doubled:
        wide = x.astype(F32)
        order_row = lax.broadcasted_iota(jnp.int32, wide.shape, 0)
        x = (wide * jnp.where(order_row == 0, 1.0, 2.0)).astype(BF16)
    value = dot(table_ref[0], x[:, :width]) + dot(table_ref[1], x[:, width:])
    if scaled:
        value = value * scale_ref[...]
    pad = out_ref.shape[2] - width
    if pad:
        value = jnp.concatenate([value, jnp.zeros((value.shape[0], pad), F32)], axis=1)
    chunks, cols, _ = out_ref.shape
    for b in range(chunks):
        out_ref[b] = value[b * cols : (b + 1) * cols].astype(BF16)


def erf(values):
    return lax.erf(values)


def mlp_kernel(
    row_groups, wide, block, grad_scale,
    recv_ref, state_ref, cot_ref, up_ref, down_ref,
    send_ref, back_ref,
    mixed, cots, active_all, back_pre_all, grads,
):
    rows, cols, channels = state_ref.shape
    chunks = recv_ref.shape[0]
    plan = (row_groups, rows, chunks, wide)
    for k in range(rows):
        smooth = take_row(plan, lambda b: recv_ref[b], k)
        mixed[pl.ds(k * cols, cols), :] = state_ref[k].astype(F32) + smooth
        cots[pl.ds(k * cols, cols), :] = cot_ref[k].astype(F32)

    def step(index, _):
        at = pl.ds(pl.multiple_of(index * block, block), block)
        up = up_ref[...]
        pre = dot(mixed[at, :].astype(BF16), up)
        back_active = dot(cots[at, :].astype(BF16), down_ref[...])
        cdf = 0.5 * (1.0 + erf(pre * (1.0 / math.sqrt(2.0))))
        density = jnp.exp(-0.5 * pre * pre) * (1.0 / math.sqrt(2.0 * math.pi))
        active_all[at, :] = (pre * cdf).astype(BF16)
        back_pre = (back_active * (cdf + pre * density)).astype(BF16)
        back_pre_all[at, :] = back_pre
        back_ref[at, :] = cots[at, :] + dot(back_pre, up, ((1,), (1,)))
        return 0

    lax.fori_loop(0, rows * cols // block, step, 0)
    up_part = dot(mixed[...].astype(BF16), back_pre_all[...], ((0,), (0,)))
    down_part = dot(cots[...].astype(BF16), active_all[...], ((0,), (0,)))
    place(grads, up_part * grad_scale, lead=(0,))
    place(grads, down_part * grad_scale, lead=(1,))

    per_band = chunks // 2
    bands = channels // per_band
    lanes = up_ref.shape[1] // 2
    for b in range(chunks):
        line = pick(grads, 2 * lanes, b // 2, bands, per_band, lead=(b % 2,)).astype(BF16)
        for half in range(2):
            send_ref[b, half * bands : (half + 1) * bands, :lanes] = line[
                :, half * lanes : (half + 1) * lanes
            ]

    def store(chunk, value):
        send_ref[chunk, 2 * bands :, :] = value

    put_tile(
        (row_groups, rows, chunks), lambda k: back_ref[pl.ds(k * cols, cols), :], store
    )


def join_kernel(row_groups, wide, recv_ref, back_ref, out_ref):
    rows, cols, _ = out_ref.shape
    plan = (row_groups, rows, recv_ref.shape[0], wide)
    for k in range(rows):
        field = take_row(plan, lambda b: recv_ref[b], k)
        out_ref[k] = (back_ref[pl.ds(k * cols, cols), :] + field).astype(BF16)


def body(state_grid, spectral_filter, up_weight, down_weight, cotangent):
    _, rows, cols, channels = state_grid.shape
    bands = lax.axis_size("lat")
    row_groups = lax.axis_size("rows")
    channel_groups = lax.axis_size("chans")
    chunks = row_groups * channel_groups
    degrees = spectral_filter.shape[0]
    hidden = up_weight.shape[1]
    lat_total, lon_total = rows * bands, cols * chunks
    groups = bands * row_groups
    orders = degrees // groups
    per = rows // row_groups
    wide = channels // channel_groups
    width = per * wide
    lanes = -(-width // 128) * 128
    lon_axes = ("chans", "rows")
    lat_axes = ("lat", "rows")
    me = lax.axis_index("lat") * row_groups + lax.axis_index("rows")

    state = state_grid.reshape(rows, cols, channels)
    cot = cotangent.reshape(rows, cols, channels)

    sent = call(
        functools.partial(split_kernel, row_groups), shaped((chunks, cols, lanes), BF16), state
    )
    whole = lax.all_to_all(sent, lon_axes, 0, 0, tiled=True)

    gains = lax.all_gather(spectral_filter, "rows", axis=1, tiled=True)
    table, table_t = fourier_tables(lon_total, groups, orders)
    p_table, pt_table = legendre_tables(me * orders, orders, lat_total, groups, degrees)
    own = lax.dynamic_slice_in_dim(row_scale(lat_total, lon_total), me * per, per)
    scale_one = jnp.broadcast_to(own[:, None], (per, wide)).reshape(1, width)
    scale_two = jnp.concatenate([scale_one, scale_one], axis=1)

    def forward(x, doubled, scale, skip):
        extra = [] if scale is None else [scale]
        return call(
            functools.partial(forward_kernel, width, doubled, scale is not None, skip),
            shaped((groups * TILE, 2 * width), BF16),
            x, table, *extra,
            scratch=[
                pltpu.VMEM((lon_total, lanes), F32),
                tiles_of(groups * TILE, 2 * width),
            ],
        )

    def turn(x):
        moved = lax.all_to_all(
            x.reshape(groups, TILE, 2 * width), lat_axes, 0, 0, tiled=True
        )
        return moved.reshape(groups * TILE, 2 * width)

    def spectral(x):
        return call(
            functools.partial(spectral_kernel, orders, per, wide),
            shaped((groups * TILE, 2 * width), BF16),
            x, p_table, pt_table, gains,
            scratch=[
                tiles_of(groups * TILE, 2 * width),
                tiles_of(groups * TILE, 2 * width),
            ],
        )

    def inverse(x, doubled, scale):
        extra = [] if scale is None else [scale]
        return call(
            functools.partial(inverse_kernel, width, doubled, scale is not None),
            shaped((chunks, cols, lanes), BF16),
            x, table_t, *extra,
        )

    modes = turn(forward(whole, False, scale_two, 0))
    waves = turn(spectral(modes))
    smooth = lax.all_to_all(inverse(waves, True, None), lon_axes, 0, 0, tiled=True)

    points = rows * cols
    grad_rows = 2 * (channels // (chunks // 2))
    sent, back_mixed = call(
        functools.partial(
            mlp_kernel, row_groups, wide, points // 6, 1.0 / math.sqrt(lat_total * lon_total)
        ),
        [shaped((chunks, grad_rows + cols, lanes), BF16), shaped((points, channels), F32)],
        smooth, state, cot, up_weight, down_weight,
        scratch=[
            pltpu.VMEM((points, channels), F32),
            pltpu.VMEM((points, channels), F32),
            pltpu.VMEM((points, hidden), BF16),
            pltpu.VMEM((points, hidden), BF16),
            pltpu.VMEM((2, -(-hidden // 128), channels, 128), F32),
        ],
    )
    whole = lax.all_to_all(sent, lon_axes, 0, 0, tiled=True)
    back_modes = turn(forward(whole, True, None, grad_rows))

    parts = back_modes.reshape(bands, row_groups, TILE, 2 * width)
    parts = lax.dynamic_index_in_dim(parts, lax.axis_index("rows"), 1, keepdims=False)
    piece = jnp.sum(parts[:, TILE - 2 :, : hidden // 2].astype(F32), axis=0)
    pieces = lax.all_gather(piece, lon_axes, axis=0, tiled=False)
    pieces = pieces.reshape(chunks // 2, 2, hidden)

    back_waves = turn(spectral(back_modes))
    field = lax.all_to_all(inverse(back_waves, False, scale_one), lon_axes, 0, 0, tiled=True)
    grad_field = call(
        functools.partial(join_kernel, row_groups, wide),
        shaped((rows, cols, channels), BF16),
        field, back_mixed,
    )
    return grad_field.reshape(state_grid.shape), pieces[:, 0], pieces[:, 1]


def solution(mesh):
    bands, tiles = mesh.shape["lat"], mesh.shape["lon"]
    fine = Mesh(
        mesh.devices.reshape(bands, tiles // ROW_GROUPS, ROW_GROUPS), ("lat", "chans", "rows")
    )
    lon = ("chans", "rows")
    placed = (P(None, "lat", lon, None), P(None, lon), P(), P(), P(None, "lat", lon, None))
    return jax.shard_map(
        body,
        mesh=fine,
        in_specs=placed,
        out_specs=(P(None, "lat", lon, None), P("lat", None), P("lat", None)),
        check_vma=False,
    )
```

```python
import functools
import math

import jax
import jax.numpy as jnp
from jax import lax
from jax.experimental import pallas as pl
from jax.experimental.pallas import tpu as pltpu
from jax.sharding import Mesh, PartitionSpec as P

L = 384
ROW_GROUPS = 4
TILE = 8
F32 = jnp.float32
BF16 = jnp.bfloat16
VMEM_LIMIT = 24 * 1024 * 1024


def dot(a, b, dims=((1,), (0,))):
    return lax.dot_general(a, b, (dims, ((), ())), preferred_element_type=F32)


def call(kernel, outs, *args, scratch=(), cost=None, in_hbm=()):
    single = not isinstance(outs, (list, tuple))
    shapes = [outs] if single else list(outs)
    result = pl.pallas_call(
        kernel,
        out_shape=shapes,
        in_specs=[pl.BlockSpec(memory_space=pltpu.VMEM)] * len(args),
        out_specs=[
            pl.BlockSpec(memory_space=pltpu.HBM if i in in_hbm else pltpu.VMEM)
            for i in range(len(shapes))
        ],
        scratch_shapes=list(scratch),
        compiler_params=pltpu.CompilerParams(vmem_limit_bytes=VMEM_LIMIT),
        cost_estimate=cost,
    )(*args)
    return result[0] if single else result


def shaped(shape, dtype):
    return jax.ShapeDtypeStruct(shape, dtype)


def tiles_of(rows, width):
    return pltpu.VMEM((-(-width // 128), rows, 128), F32)


def pick(ref, width, start=0, size=None, stride=1, lead=()):
    tiles = -(-width // 128)
    at = slice(None) if size is None else pl.ds(start, size, stride=stride)
    value = jnp.concatenate([ref[(*lead, i, at, slice(None))] for i in range(tiles)], axis=1)
    return value[:, :width] if tiles * 128 > width else value


def place(ref, value, start=0, size=None, stride=1, lead=()):
    pad = -value.shape[1] % 128
    if pad:
        value = jnp.concatenate([value, jnp.zeros((value.shape[0], pad), value.dtype)], axis=1)
    at = slice(None) if size is None else pl.ds(start, size, stride=stride)
    for i in range(value.shape[1] // 128):
        ref[(*lead, i, at, slice(None))] = value[:, i * 128 : (i + 1) * 128]


def row_scale(lat_total, lon_total):
    colatitude = (jnp.arange(lat_total, dtype=F32) + 0.5) * (math.pi / lat_total)
    counter = jnp.arange(1, lat_total // 2 + 1, dtype=F32)
    series = jnp.sum(
        jnp.cos(2.0 * counter[None, :] * colatitude[:, None])
        / (4.0 * counter * counter - 1.0)[None, :],
        axis=1,
    )
    return 2.0 / lat_total * (1.0 - 2.0 * series) * (2.0 * math.pi / lon_total)


def wave_pair(product, lon_total):
    quarter = lon_total // 4
    turns = jnp.floor(product * (1.0 / quarter) + 0.5)
    angle = (product - turns * quarter) * (2.0 * math.pi / lon_total)
    square = angle * angle
    sine = angle * (
        1.0 + square * (-1.0 / 6 + square * (1.0 / 120 + square * (-1.0 / 5040 + square / 362880)))
    )
    cosine = 1.0 + square * (
        -0.5 + square * (1.0 / 24 + square * (-1.0 / 720 + square / 40320))
    )
    quadrant = turns - 4.0 * jnp.floor(turns * 0.25)
    odd = (quadrant == 1.0) | (quadrant == 3.0)
    first = jnp.where(odd, sine, cosine)
    second = jnp.where(odd, cosine, sine)
    first = jnp.where((quadrant == 1.0) | (quadrant == 2.0), -first, first)
    second = jnp.where(quadrant >= 2.0, -second, second)
    return first, second


def fourier_kernel(per_group, table_out, turned_out, table_ref, turned_ref, sems):
    _, padded, lon_total = table_ref.shape

    def fill(ref, start, turn, live):
        here = wave_pair(start, lon_total)
        turn_cos, turn_sin = wave_pair(turn, lon_total)

        def ahead(pair):
            cosine, sine = pair
            return cosine * turn_cos - sine * turn_sin, sine * turn_cos + cosine * turn_sin

        def step(index, pair):
            later = ahead(pair)
            at = pl.ds(pl.multiple_of(index * 2 * TILE, 2 * TILE), 2 * TILE)
            for p, sign in enumerate((1.0, -1.0)):
                both = jnp.concatenate([pair[p], later[p]], axis=0)
                ref[p, at, :] = jnp.where(live, sign * both, 0.0).astype(BF16)
            return ahead(later)

        lax.fori_loop(0, ref.shape[1] // (2 * TILE), step, here)

    def whole(shape, axis):
        return lax.broadcasted_iota(jnp.int32, shape, axis)

    shape = (TILE, lon_total)
    lon_index = whole(shape, 1).astype(F32)
    rank = whole((2 * TILE, lon_total), 0) % TILE
    fill(table_ref, whole(shape, 0).astype(F32) * lon_index, per_group * lon_index, rank < per_group)
    first = pltpu.make_async_copy(table_ref, table_out, sems.at[0])
    first.start()

    shape = (TILE, padded)
    column = whole(shape, 1)
    order = (column // TILE * per_group + column % TILE).astype(F32)
    rank = whole((2 * TILE, padded), 1) % TILE
    fill(turned_ref, whole(shape, 0).astype(F32) * order, TILE * order, rank < per_group)
    second = pltpu.make_async_copy(turned_ref, turned_out, sems.at[1])
    second.start()
    first.wait()
    second.wait()


def fourier_tables(lon_total, groups, per_group):
    padded = groups * TILE
    shapes = [(2, padded, lon_total), (2, lon_total, padded)]
    return call(
        functools.partial(fourier_kernel, per_group),
        [shaped(shape, BF16) for shape in shapes],
        scratch=[pltpu.VMEM(shape, BF16) for shape in shapes] + [pltpu.SemaphoreType.DMA((2,))],
        cost=pl.CostEstimate(
            flops=30 * padded * lon_total, bytes_accessed=8 * padded * lon_total, transcendentals=0
        ),
        in_hbm=(0, 1),
    )


def legendre_kernel(
    orders, degrees, m_ref, cos_ref, diag_ref, p_out, pt_out, table, p_ref, pt_ref, sems
):
    m = m_ref[...]
    squares = m * m
    cosine = cos_ref[...]
    diag = diag_ref[...]

    def block(index, carry):
        here, before, scale = carry
        level = jnp.exp(diag + scale)
        for inner in range(TILE):
            degree = index * TILE + inner
            lv = jnp.full(m.shape, degree, jnp.int32).astype(F32)
            spread = jnp.maximum(lv * lv - squares, 1.0)
            growth = jnp.sqrt(jnp.maximum(4.0 * lv * lv - 1.0, 1.0) / spread)
            low = lv - 1.0
            damping = jnp.sqrt(
                jnp.maximum(low * low - squares, 0.0) / jnp.maximum(4.0 * low * low - 1.0, 1.0)
            )
            ahead = growth * cosine * here - growth * damping * before
            live = lv > m
            here, before = jnp.where(live, ahead, here), jnp.where(live, here, before)
            values = jnp.where(lv >= m, level * here, 0.0)
            place(table, values, pl.multiple_of(degree * TILE, TILE), TILE)
        largest = jnp.maximum(jnp.abs(here), jnp.abs(before))
        return here / largest, before / largest, scale + jnp.log(largest)

    ones = jnp.ones(m.shape, F32)
    zeros = jnp.zeros(m.shape, F32)
    lax.fori_loop(0, degrees // TILE, block, (ones, zeros, zeros))
    copies = []
    for r in range(orders):
        rows = pick(table, m.shape[1], r, degrees, TILE)
        p_ref[r] = rows.astype(BF16)
        pt_ref[r] = rows.T.astype(BF16)
        copies += [
            pltpu.make_async_copy(p_ref.at[r], p_out.at[r], sems.at[0, r]),
            pltpu.make_async_copy(pt_ref.at[r], pt_out.at[r], sems.at[1, r]),
        ]
        copies[-2].start()
        copies[-1].start()
    for copy in copies:
        copy.wait()


def legendre_tables(first_order, orders, lat_total, groups, degrees):
    per = lat_total // groups
    half = lat_total // 2
    position = jnp.arange(lat_total, dtype=jnp.int32)
    row = position % groups * per + position // groups
    north = jnp.minimum(row, lat_total - 1 - row)
    colatitude = (north.astype(F32) + 0.5) * (math.pi / lat_total)
    cosine = jnp.where(row < half, 1.0, -1.0) * jnp.cos(colatitude)
    log_sine = jnp.log(jnp.sin(colatitude))
    later = jnp.arange(1, degrees, dtype=F32)
    ratios = jnp.log((2.0 * later - 1.0) / (2.0 * later))
    order = (first_order + jnp.arange(TILE, dtype=jnp.int32)).astype(F32)
    partial_logs = jnp.sum(jnp.where(later[None, :] <= order[:, None], ratios[None, :], 0.0), axis=1)
    base_logs = 0.5 * (jnp.log((2.0 * order + 1.0) / (4.0 * math.pi)) + partial_logs)
    shape = (TILE, lat_total)
    diag = base_logs[:, None] + order[:, None] * log_sine[None, :]
    return call(
        functools.partial(legendre_kernel, orders, degrees),
        [
            shaped((orders, degrees, lat_total), BF16),
            shaped((orders, lat_total, degrees), BF16),
        ],
        jnp.broadcast_to(order[:, None], shape),
        jnp.broadcast_to(cosine[None, :], shape),
        diag,
        scratch=[
            tiles_of(degrees * TILE, lat_total),
            pltpu.VMEM((orders, degrees, lat_total), BF16),
            pltpu.VMEM((orders, lat_total, degrees), BF16),
            pltpu.SemaphoreType.DMA((2, orders)),
        ],
        in_hbm=(0, 1),
        cost=pl.CostEstimate(flops=40_000_000, bytes_accessed=4_000_000, transcendentals=1_000_000),
    )


def chunk_lanes(cols, width):
    return -(-(cols // TILE * width) // 128) * 128


def put_tile(plan, load, store):
    row_groups, rows, chunks, wide = plan
    per = rows // row_groups
    for q in range(row_groups):
        lines = [load(q * per + k).astype(F32) for k in range(per)]
        cols = lines[0].shape[0]
        used = cols // TILE * per * wide
        pad = chunk_lanes(cols, per * wide) - used
        for g in range(chunks // row_groups):
            parts = [
                line[j : j + TILE, g * wide : (g + 1) * wide]
                for j in range(0, cols, TILE)
                for line in lines
            ]
            if pad:
                parts.append(jnp.zeros((TILE, pad), F32))
            store(g * row_groups + q, jnp.concatenate(parts, axis=1).astype(BF16))


def take_row(plan, cols, load_chunk, k):
    row_groups, rows, chunks, wide = plan
    per = rows // row_groups
    q, inner = k // per, k % per
    held = [load_chunk(g * row_groups + q) for g in range(chunks // row_groups)]
    lines = []
    for j in range(cols // TILE):
        at = (j * per + inner) * wide
        lines.append(jnp.concatenate([one[:, at : at + wide] for one in held], axis=1))
    return jnp.concatenate(lines, axis=0)


def split_kernel(plan, x_ref, out_ref):
    def store(chunk, value):
        out_ref[chunk] = value

    put_tile(plan, lambda k: x_ref[k], store)


def forward_kernel(width, cols, doubled, scaled, skip, *refs):
    if scaled:
        x_ref, table_ref, scale_ref, filter_ref, out_ref, x_all, out_all = refs
    else:
        x_ref, table_ref, out_ref, x_all, out_all = refs
    chunks = x_ref.shape[0]
    used = chunk_lanes(cols, width)
    for b in range(chunks):
        chunk = x_ref[b, :, :used].astype(F32)
        for j in range(cols // TILE):
            x_all[pl.ds(b * cols + j * TILE, TILE), :] = chunk[:, j * width : (j + 1) * width]
    x = x_all[...].astype(BF16)
    value = jnp.concatenate([dot(table_ref[p], x) for p in range(2)], axis=1)
    if scaled:
        value = value * scale_ref[...]
    if doubled:
        order_row = lax.broadcasted_iota(jnp.int32, value.shape, 0)
        value = value * jnp.where(order_row == 0, 1.0, 2.0)
    place(out_all, value)
    if scaled:
        gains = filter_ref[...]
        parts = []
        for _ in range(3):
            parts.append(gains.astype(BF16).astype(F32))
            gains = gains - parts[-1]
        groups = value.shape[0] // TILE
        shape = (groups, value.shape[1])
        upper = jnp.concatenate(parts[:2], axis=1)
        lower = jnp.concatenate([parts[2], jnp.zeros_like(parts[2])], axis=1)
        place(out_all, jnp.broadcast_to(upper, shape), TILE - 2, groups, TILE)
        place(out_all, jnp.broadcast_to(lower, shape), TILE - 1, groups, TILE)
    if skip:
        lanes, bands = skip
        total = x_ref[0, :, used:].astype(F32)
        for b in range(1, chunks):
            total = total + x_ref[b, :, used:].astype(F32)
        groups = value.shape[0] // TILE
        per = bands // (total.shape[1] // (2 * lanes))
        for high in range(bands // per):
            for half in range(2):
                at = (2 * high + half) * lanes
                for q in range(groups // bands):
                    place(
                        out_all,
                        total[:per, at : at + lanes],
                        (high * per * (groups // bands) + q) * TILE + TILE - 2 + half,
                        per,
                        groups // bands * TILE,
                    )
    out_ref[...] = pick(out_all, value.shape[1]).astype(BF16)


def gather_gains(x_all, bands, width):
    groups = x_all.shape[1] // TILE
    row_groups = groups // bands
    parts = []
    for q in range(row_groups):
        upper = pick(x_all, 2 * width, q * TILE + TILE - 2, bands, row_groups * TILE)
        lower = pick(x_all, width, q * TILE + TILE - 1, bands, row_groups * TILE)
        parts.append(upper[:, :width] + upper[:, width:] + lower)
    return parts


def spectral_kernel(orders, per, wide, bands, first, *refs):
    if first:
        x_ref, p_ref, pt_ref, out_ref, gain_ref, x_all, out_all = refs
    else:
        x_ref, p_ref, pt_ref, gain_ref, out_ref, piece_ref, x_all, out_all = refs
    groups = x_ref.shape[0] // TILE
    place(x_all, x_ref[...].astype(F32))
    row_groups = groups // bands
    if first:
        parts = gather_gains(x_all, bands, per * wide)
        own = wide // row_groups
        rows = []
        for at in range(0, per * wide, own):
            line = [part[:, at : at + own] for part in parts]
            rows.append(jnp.concatenate(line + line, axis=1))
        gains = jnp.concatenate(rows, axis=0)
        gain_ref[...] = gains
    else:
        gains = gain_ref[...]
        mine = lax.axis_index("rows")
        lanes = piece_ref.shape[1]
        for half in range(2):
            sums = pick(x_all, lanes, mine * TILE + TILE - 2 + half, bands, row_groups * TILE)
            piece_ref[half : half + 1, :] = jnp.sum(sums, axis=0, keepdims=True)
    half = per * wide
    for r in range(orders):
        rows = pick(x_all, 2 * half, r, groups, TILE)
        modes = jnp.concatenate(
            [
                jnp.concatenate(
                    [rows[:, p * half + k * wide : p * half + (k + 1) * wide] for p in range(2)],
                    axis=1,
                )
                for k in range(per)
            ],
            axis=0,
        ).astype(BF16)
        spectrum = dot(p_ref[r], modes)
        filtered = (spectrum * gains).astype(BF16)
        waves = dot(pt_ref[r], filtered)
        parts = []
        for p in range(2):
            for k in range(per):
                parts.append(waves[k * groups : (k + 1) * groups, p * wide : (p + 1) * wide])
        place(out_all, jnp.concatenate(parts, axis=1), r, groups, TILE)
    for r in range(orders, TILE):
        place(out_all, jnp.zeros((groups, 2 * half), F32), r, groups, TILE)
    out_ref[...] = pick(out_all, 2 * half).astype(BF16)


def inverse_kernel(width, cols, doubled, scaled, *refs):
    if scaled:
        x_ref, table_ref, scale_ref, piece_ref, out_ref = refs
    else:
        x_ref, table_ref, out_ref = refs
    x = x_ref[...]
    if doubled:
        wide = x.astype(F32)
        order_row = lax.broadcasted_iota(jnp.int32, wide.shape, 0)
        x = (wide * jnp.where(order_row == 0, 1.0, 2.0)).astype(BF16)
    value = dot(table_ref[0], x[:, :width]) + dot(table_ref[1], x[:, width:])
    chunks, _, lanes = out_ref.shape
    pad = lanes - cols // TILE * width
    rest = jnp.zeros((TILE, pad), F32)
    if scaled:
        value = value * scale_ref[...]
        piece = piece_ref[...]
        share = 2 * piece.shape[1] // TILE
        rest = jnp.concatenate(
            [piece[i * share // piece.shape[1] : i * share // piece.shape[1] + 1,
                   i * share % piece.shape[1] : i * share % piece.shape[1] + share]
             for i in range(TILE)],
            axis=0,
        )
        if pad > share:
            rest = jnp.concatenate([rest, jnp.zeros((TILE, pad - share), F32)], axis=1)
    for b in range(chunks):
        lines = [
            value[b * cols + j * TILE : b * cols + (j + 1) * TILE] for j in range(cols // TILE)
        ]
        out_ref[b] = jnp.concatenate(lines + [rest], axis=1).astype(BF16)


def erf(values):
    return lax.erf(values)


def mlp_kernel(
    row_groups, wide, block, grad_scale,
    recv_ref, state_ref, cot_ref, up_ref, down_ref,
    send_ref, back_out,
    mixed, cots, active_all, back_pre_all, grads, back_ref, sem,
):
    rows, cols, channels = state_ref.shape
    chunks = recv_ref.shape[0]
    plan = (row_groups, rows, chunks, wide)
    for k in range(rows):
        smooth = take_row(plan, cols, lambda b: recv_ref[b].astype(F32), k)
        mixed[pl.ds(k * cols, cols), :] = state_ref[k].astype(F32) + smooth
        cots[pl.ds(k * cols, cols), :] = cot_ref[k].astype(F32)

    def step(index, _):
        at = pl.ds(pl.multiple_of(index * block, block), block)
        up = up_ref[...]
        pre = dot(mixed[at, :].astype(BF16), up)
        back_active = dot(cots[at, :].astype(BF16), down_ref[...])
        cdf = 0.5 * (1.0 + erf(pre * (1.0 / math.sqrt(2.0))))
        density = jnp.exp(-0.5 * pre * pre) * (1.0 / math.sqrt(2.0 * math.pi))
        active_all[at, :] = (pre * cdf).astype(BF16)
        back_pre = (back_active * (cdf + pre * density)).astype(BF16)
        back_pre_all[at, :] = back_pre
        back_ref[at, :] = cots[at, :] + dot(back_pre, up, ((1,), (1,)))
        return 0

    lax.fori_loop(0, rows * cols // block, step, 0)
    kept = pltpu.make_async_copy(back_ref, back_out, sem)
    kept.start()
    up_part = dot(mixed[...].astype(BF16), back_pre_all[...], ((0,), (0,)))
    down_part = dot(cots[...].astype(BF16), active_all[...], ((0,), (0,)))
    place(grads, up_part * grad_scale, lead=(0,))
    place(grads, down_part * grad_scale, lead=(1,))

    per_band = chunks // 2
    bands = channels // per_band
    lanes = up_ref.shape[1] // 2
    used = chunk_lanes(cols, rows // row_groups * wide)
    for b in range(chunks):
        line = pick(grads, 2 * lanes, b // 2, bands, per_band, lead=(b % 2,)).astype(BF16)
        for high in range(0, bands, TILE):
            send_ref[b, : min(TILE, bands), used + high // TILE * 2 * lanes : used + (high // TILE + 1) * 2 * lanes] = line[
                high : high + TILE
            ]

    def store(chunk, value):
        send_ref[chunk, :, :used] = value

    put_tile(plan, lambda k: back_ref[pl.ds(k * cols, cols), :], store)
    kept.wait()


def join_kernel(row_groups, wide, recv_ref, back_ref, out_ref, up_ref, down_ref, held):
    rows, cols, _ = out_ref.shape
    chunks = recv_ref.shape[0]
    plan = (row_groups, rows, chunks, wide)
    for k in range(rows):
        field = take_row(plan, cols, lambda b: recv_ref[b].astype(F32), k)
        out_ref[k] = (back_ref[pl.ds(k * cols, cols), :] + field).astype(BF16)
    used = cols // TILE * (rows // row_groups) * wide
    lines, hidden = up_ref.shape
    share = hidden // TILE
    for b in range(chunks):
        held[pl.ds(b * TILE, TILE), :] = jnp.concatenate(
            [recv_ref[b, :, used : used + share].astype(F32), jnp.zeros((TILE, 128 - share), F32)],
            axis=1,
        )
    for parity, ref in enumerate((up_ref, down_ref)):
        ref[...] = jnp.concatenate(
            [
                held[pl.ds(parity * TILE + i, lines, stride=2 * TILE), :][:, :share]
                for i in range(TILE)
            ],
            axis=1,
        )


def body(state_grid, spectral_filter, up_weight, down_weight, cotangent):
    _, rows, cols, channels = state_grid.shape
    bands = lax.axis_size("lat")
    row_groups = lax.axis_size("rows")
    channel_groups = lax.axis_size("chans")
    chunks = row_groups * channel_groups
    degrees = spectral_filter.shape[0]
    hidden = up_weight.shape[1]
    lat_total, lon_total = rows * bands, cols * chunks
    groups = bands * row_groups
    orders = degrees // groups
    per = rows // row_groups
    wide = channels // channel_groups
    width = per * wide
    lanes = chunk_lanes(cols, width)
    plan = (row_groups, rows, chunks, wide)
    lon_axes = ("chans", "rows")
    lat_axes = ("lat", "rows")
    me = lax.axis_index("lat") * row_groups + lax.axis_index("rows")

    state = state_grid.reshape(rows, cols, channels)
    cot = cotangent.reshape(rows, cols, channels)

    sent = call(
        functools.partial(split_kernel, plan), shaped((chunks, TILE, lanes), BF16), state
    )
    whole = lax.all_to_all(sent, lon_axes, 0, 0, tiled=True)

    shared = lax.dynamic_index_in_dim(
        spectral_filter.reshape(degrees // bands, bands, channels // chunks),
        lax.axis_index("lat"), 1, keepdims=False,
    ).reshape(1, width)
    table, table_t = fourier_tables(lon_total, groups, orders)
    p_table, pt_table = legendre_tables(me * orders, orders, lat_total, groups, degrees)
    own = lax.dynamic_slice_in_dim(row_scale(lat_total, lon_total), me * per, per)
    scale_one = jnp.broadcast_to(own[:, None], (per, wide)).reshape(1, width)
    scale_two = jnp.concatenate([scale_one, scale_one], axis=1)

    def forward(x, doubled, skip, *extra):
        return call(
            functools.partial(forward_kernel, width, cols, doubled, bool(extra), skip),
            shaped((groups * TILE, 2 * width), BF16),
            x, table, *extra,
            scratch=[
                pltpu.VMEM((lon_total, width), F32),
                tiles_of(groups * TILE, 2 * width),
            ],
        )

    def turn(x):
        moved = lax.all_to_all(
            x.reshape(groups, TILE, 2 * width), lat_axes, 0, 0, tiled=True
        )
        return moved.reshape(groups * TILE, 2 * width)

    def spectral(x, *gains):
        extra = shaped((2, hidden // 2), F32) if gains else shaped((degrees, 2 * wide), F32)
        return call(
            functools.partial(spectral_kernel, orders, per, wide, bands, not gains),
            [shaped((groups * TILE, 2 * width), BF16), extra],
            x, p_table, pt_table, *gains,
            scratch=[
                tiles_of(groups * TILE, 2 * width),
                tiles_of(groups * TILE, 2 * width),
            ],
        )

    def inverse(x, doubled, *extra):
        return call(
            functools.partial(inverse_kernel, width, cols, doubled, bool(extra)),
            shaped((chunks, TILE, lanes), BF16),
            x, table_t, *extra,
        )

    modes = turn(forward(whole, False, None, scale_two, shared))
    filtered, gains = spectral(modes)
    waves = turn(filtered)
    smooth = lax.all_to_all(inverse(waves, True), lon_axes, 0, 0, tiled=True)

    points = rows * cols
    grad_lanes = hidden * -(-bands // TILE)
    sent, back_mixed = call(
        functools.partial(
            mlp_kernel, row_groups, wide, points // 6, 1.0 / math.sqrt(lat_total * lon_total)
        ),
        [shaped((chunks, TILE, lanes + grad_lanes), BF16), shaped((points, channels), F32)],
        smooth, state, cot, up_weight, down_weight,
        in_hbm=(1,),
        scratch=[
            pltpu.VMEM((points, channels), F32),
            pltpu.VMEM((points, channels), F32),
            pltpu.VMEM((points, hidden), BF16),
            pltpu.VMEM((points, hidden), BF16),
            pltpu.VMEM((2, -(-hidden // 128), channels, 128), F32),
            pltpu.VMEM((points, channels), F32),
            pltpu.SemaphoreType.DMA,
        ],
    )
    whole = lax.all_to_all(sent, lon_axes, 0, 0, tiled=True)
    back_modes = turn(forward(whole, True, (hidden // 2, bands)))
    filtered, piece = spectral(back_modes, gains)
    back_waves = turn(filtered)
    field = lax.all_to_all(
        inverse(back_waves, False, scale_one, piece), lon_axes, 0, 0, tiled=True
    )
    grad_field, grad_up, grad_down = call(
        functools.partial(join_kernel, row_groups, wide),
        [
            shaped((rows, cols, channels), BF16),
            shaped((chunks // 2, hidden), F32),
            shaped((chunks // 2, hidden), F32),
        ],
        field, back_mixed,
        scratch=[pltpu.VMEM((chunks * TILE, 128), F32)],
    )
    return grad_field.reshape(state_grid.shape), grad_up, grad_down


def solution(mesh):
    bands, tiles = mesh.shape["lat"], mesh.shape["lon"]
    fine = Mesh(
        mesh.devices.reshape(bands, tiles // ROW_GROUPS, ROW_GROUPS), ("lat", "chans", "rows")
    )
    lon = ("chans", "rows")
    placed = (P(None, "lat", lon, None), P(None, lon), P(), P(), P(None, "lat", lon, None))
    return jax.shard_map(
        body,
        mesh=fine,
        in_specs=placed,
        out_specs=(P(None, "lat", lon, None), P("lat", None), P("lat", None)),
        check_vma=False,
    )
```

```python
import functools
import math

import jax
import jax.numpy as jnp
from jax import lax
from jax.experimental import pallas as pl
from jax.experimental.pallas import tpu as pltpu
from jax.sharding import PartitionSpec as P

TILE = 8
F32 = jnp.float32
BF16 = jnp.bfloat16
VMEM_LIMIT = 24 * 1024 * 1024


def dot(a, b, dims=((1,), (0,))):
    return lax.dot_general(a, b, (dims, ((), ())), preferred_element_type=F32)


def call(kernel, outs, *args, scratch=(), cost=None, in_hbm=()):
    single = not isinstance(outs, (list, tuple))
    shapes = [outs] if single else list(outs)
    result = pl.pallas_call(
        kernel,
        out_shape=shapes,
        in_specs=[pl.BlockSpec(memory_space=pltpu.VMEM)] * len(args),
        out_specs=[
            pl.BlockSpec(memory_space=pltpu.HBM if i in in_hbm else pltpu.VMEM)
            for i in range(len(shapes))
        ],
        scratch_shapes=list(scratch),
        compiler_params=pltpu.CompilerParams(vmem_limit_bytes=VMEM_LIMIT),
        cost_estimate=cost,
    )(*args)
    return result[0] if single else result


def shaped(shape, dtype):
    return jax.ShapeDtypeStruct(shape, dtype)


def tiles_of(rows, width):
    return pltpu.VMEM((-(-width // 128), rows, 128), F32)


def pick(ref, width, start=0, size=None, stride=1, lead=()):
    tiles = -(-width // 128)
    at = slice(None) if size is None else pl.ds(start, size, stride=stride)
    value = jnp.concatenate([ref[(*lead, i, at, slice(None))] for i in range(tiles)], axis=1)
    return value[:, :width] if tiles * 128 > width else value


def place(ref, value, start=0, size=None, stride=1, lead=()):
    pad = -value.shape[1] % 128
    if pad:
        value = jnp.concatenate([value, jnp.zeros((value.shape[0], pad), value.dtype)], axis=1)
    at = slice(None) if size is None else pl.ds(start, size, stride=stride)
    for i in range(value.shape[1] // 128):
        ref[(*lead, i, at, slice(None))] = value[:, i * 128 : (i + 1) * 128]


def row_scale(lat_total, lon_total):
    colatitude = (jnp.arange(lat_total, dtype=F32) + 0.5) * (math.pi / lat_total)
    counter = jnp.arange(1, lat_total // 2 + 1, dtype=F32)
    series = jnp.sum(
        jnp.cos(2.0 * counter[None, :] * colatitude[:, None])
        / (4.0 * counter * counter - 1.0)[None, :],
        axis=1,
    )
    return 2.0 / lat_total * (1.0 - 2.0 * series) * (2.0 * math.pi / lon_total)


def wave_pair(product, lon_total):
    quarter = lon_total // 4
    turns = jnp.floor(product * (1.0 / quarter) + 0.5)
    angle = (product - turns * quarter) * (2.0 * math.pi / lon_total)
    square = angle * angle
    sine = angle * (
        1.0 + square * (-1.0 / 6 + square * (1.0 / 120 + square * (-1.0 / 5040 + square / 362880)))
    )
    cosine = 1.0 + square * (
        -0.5 + square * (1.0 / 24 + square * (-1.0 / 720 + square / 40320))
    )
    quadrant = turns - 4.0 * jnp.floor(turns * 0.25)
    odd = (quadrant == 1.0) | (quadrant == 3.0)
    first = jnp.where(odd, sine, cosine)
    second = jnp.where(odd, cosine, sine)
    first = jnp.where((quadrant == 1.0) | (quadrant == 2.0), -first, first)
    second = jnp.where(quadrant >= 2.0, -second, second)
    return first, second


def rotate(pair, turn):
    cosine, sine = pair
    turn_cos, turn_sin = turn
    return cosine * turn_cos - sine * turn_sin, sine * turn_cos + cosine * turn_sin


def phased(product, part, lon_total):
    cosine, sine = wave_pair(product, lon_total)
    return jnp.where(part == 1, -sine, cosine), jnp.where(part == 1, cosine, sine)


def fourier_kernel(bands, orders, table_out, turned_out, table_ref, turned_ref, sems):
    lon_total, modes = table_ref.shape
    per = 2 * orders

    shape = (TILE, modes)
    column = lax.broadcasted_iota(jnp.int32, shape, 1)
    group = column // per
    rank = column - group * per
    order = (bands * (rank // 2) + group).astype(F32)
    row = lax.broadcasted_iota(jnp.int32, shape, 0).astype(F32)
    turn = wave_pair(TILE * order, lon_total)

    def step(index, pair):
        later = rotate(pair, turn)
        at = pl.ds(pl.multiple_of(index * 2 * TILE, 2 * TILE), 2 * TILE)
        table_ref[at, :] = jnp.concatenate([pair[0], later[0]], axis=0).astype(BF16)
        return rotate(later, turn)

    lax.fori_loop(0, lon_total // (2 * TILE), step, phased(row * order, rank % 2, lon_total))
    first = pltpu.make_async_copy(table_ref, table_out, sems.at[0])
    first.start()

    shape = (TILE, lon_total)
    lon_index = lax.broadcasted_iota(jnp.int32, shape, 1).astype(F32)
    row = lax.broadcasted_iota(jnp.int32, shape, 0)
    start = phased((bands * (row // 2)).astype(F32) * lon_index, row % 2, lon_total)
    inner = wave_pair(TILE // 2 * bands * lon_index, lon_total)
    outer = wave_pair(lon_index, lon_total)

    def group_step(t, pair):
        now = pair
        for i in range(per // (2 * TILE)):
            later = rotate(now, inner)
            at = pl.ds(pl.multiple_of(t * per + i * 2 * TILE, 2 * TILE), 2 * TILE)
            turned_ref[at, :] = jnp.concatenate([now[0], later[0]], axis=0).astype(BF16)
            now = rotate(later, inner)
        return rotate(pair, outer)

    lax.fori_loop(0, modes // per, group_step, start)
    second = pltpu.make_async_copy(turned_ref, turned_out, sems.at[1])
    second.start()
    first.wait()
    second.wait()


def fourier_tables(lon_total, bands, orders):
    modes = 2 * bands * orders
    shapes = [(lon_total, modes), (modes, lon_total)]
    return call(
        functools.partial(fourier_kernel, bands, orders),
        [shaped(shape, BF16) for shape in shapes],
        scratch=[pltpu.VMEM(shape, BF16) for shape in shapes] + [pltpu.SemaphoreType.DMA((2,))],
        cost=pl.CostEstimate(
            flops=30 * modes * lon_total, bytes_accessed=8 * modes * lon_total, transcendentals=0
        ),
        in_hbm=(0, 1),
    )


def legendre_kernel(bands, degrees, cos_ref, diag_ref, out_ref, *tables):
    tiles = diag_ref.shape[0] // TILE
    band = lax.axis_index("lat")
    cosine = cos_ref[...]
    width = cosine.shape[1]
    shape = (TILE, 128)
    rank = lax.broadcasted_iota(jnp.int32, shape, 0)
    orders = [(bands * (TILE * g + rank) + band).astype(F32) for g in range(tiles)]
    diags = [diag_ref[g * TILE : (g + 1) * TILE, :] for g in range(tiles)]

    def spread(value):
        return jnp.concatenate([value] * (-(-width // 128)), axis=1)[:, :width]

    def block(active, index, carry):
        carry = list(carry)
        for g in range(active):
            here, before, scale, inverse = carry[g]
            order = orders[g]
            square = order * order
            wide_order = spread(order)
            level = jnp.exp(diags[g] + scale)
            for inner in range(TILE):
                degree = index * TILE + inner
                lv = jnp.full(shape, degree, jnp.int32).astype(F32)
                now = jnp.sqrt(jnp.maximum(lv * lv - square, 0.0) / jnp.maximum(4.0 * lv * lv - 1.0, 1.0))
                live = lv > order
                growth = 1.0 / jnp.where(live, now, 1.0)
                ahead = spread(growth) * cosine * here - spread(growth * inverse) * before
                wide_live = spread(lv) > wide_order
                here, before = jnp.where(wide_live, ahead, here), jnp.where(wide_live, here, before)
                values = jnp.where(spread(lv) >= wide_order, level * here, 0.0)
                at = pl.multiple_of((degree - bands * TILE * g) * TILE, TILE)
                place(tables[g], values, at, TILE)
                inverse = now
            largest = jnp.maximum(jnp.abs(here), jnp.abs(before))
            carry[g] = (here / largest, before / largest, scale + jnp.log(largest), inverse)
        return tuple(carry)

    ones = jnp.ones((TILE, width), F32)
    zeros = jnp.zeros((TILE, width), F32)
    carry = tuple((ones, zeros, zeros, jnp.zeros(shape, F32)) for _ in range(tiles))
    for g in range(tiles):
        last = bands * (g + 1) if g + 1 < tiles else degrees // TILE
        carry = lax.fori_loop(bands * g, last, functools.partial(block, g + 1), carry)
    at = 0
    for g in range(tiles):
        depth = degrees - bands * TILE * g
        for r in range(TILE):
            rows = pick(tables[g], width, r, depth, TILE)
            out_ref[:, at : at + depth] = rows.T.astype(BF16)
            at += depth


def legendre_tables(bands, orders, lat_total, degrees):
    half = lat_total // 2
    colatitude = (jnp.arange(half, dtype=F32) + 0.5) * (math.pi / lat_total)
    cosine = jnp.cos(colatitude)
    log_sine = jnp.log(jnp.sin(colatitude))
    later = jnp.arange(1, degrees, dtype=F32)
    ratios = jnp.log((2.0 * later - 1.0) / (2.0 * later))
    order = (bands * jnp.arange(orders, dtype=jnp.int32) + lax.axis_index("lat")).astype(F32)
    partial_logs = jnp.sum(jnp.where(later[None, :] <= order[:, None], ratios[None, :], 0.0), axis=1)
    base_logs = 0.5 * (jnp.log((2.0 * order + 1.0) / (4.0 * math.pi)) + partial_logs)
    diag = base_logs[:, None] + order[:, None] * log_sine[None, :]
    depths = [degrees - bands * TILE * g for g in range(orders // TILE)]
    return call(
        functools.partial(legendre_kernel, bands, degrees),
        shaped((half, TILE * sum(depths)), BF16),
        jnp.broadcast_to(cosine[None, :], (TILE, half)),
        diag,
        scratch=[tiles_of(depth * TILE, half) for depth in depths],
        cost=pl.CostEstimate(flops=40_000_000, bytes_accessed=6_000_000, transcendentals=1_000_000),
    )


def slot_row(slot, rows):
    south = lax.axis_index("lat") * 2 >= lax.axis_size("lat")
    return jnp.where(south, rows - 1 - slot, slot)


def padded(count):
    return -(-count // 128) * 128


def send_tile(ref, grid, used):
    turned = grid.T
    pad = used - turned.shape[1]
    if pad:
        turned = jnp.concatenate([turned, jnp.zeros((turned.shape[0], pad), F32)], axis=1)
    for b in range(ref.shape[0]):
        ref[b, :, :used] = turned[b * TILE : (b + 1) * TILE].astype(BF16)


def take_tile(ref, points):
    chunks = [ref[b].astype(F32) for b in range(ref.shape[0])]
    return jnp.concatenate(chunks, axis=0).T[:points]


def split_kernel(x_ref, out_ref, grid):
    rows, cols, _ = x_ref.shape
    for s in range(rows):
        grid[pl.ds(s * cols, cols), :] = x_ref[slot_row(s, rows)].astype(F32)
    send_tile(out_ref, grid[...], out_ref.shape[2])


def forward_kernel(rows, cols, doubled, scaled, skip, *refs):
    if scaled:
        x_ref, table_ref, scale_ref, out_ref, x_all, out_all = refs
    else:
        x_ref, table_ref, out_ref, x_all, out_all = refs
    chunks = x_ref.shape[0]
    used = padded(rows * cols)
    held = [x_ref[b, :, :used].astype(F32) for b in range(chunks)]
    for s in range(rows):
        x_all[pl.ds(s * TILE, TILE), :] = jnp.concatenate(
            [one[:, s * cols : (s + 1) * cols] for one in held], axis=1
        )
    value = dot(x_all[...].astype(BF16), table_ref[...])
    if scaled:
        value = value * scale_ref[...]
    if doubled:
        column = lax.broadcasted_iota(jnp.int32, value.shape, 1)
        value = value * jnp.where(column < 2, 1.0, 2.0)
    modes = value.shape[1]
    place(out_all, value)
    lines = [pick(out_all, modes, c, rows, TILE) for c in range(TILE)]
    bands = out_ref.shape[0]
    per = modes // bands
    share = 2 * TILE
    for t in range(bands):
        for g in range(per // share):
            at = t * per + g * share
            tile = jnp.concatenate([line[:, at : at + share] for line in lines], axis=1).astype(BF16)
            for i in range(rows // TILE):
                lane = i * TILE * per + g * 128
                out_ref[t, :, lane : lane + 128] = tile[i * TILE : (i + 1) * TILE]
    if skip:
        total = x_ref[0, :, used:].astype(F32)
        for b in range(1, chunks):
            total = total + x_ref[b, :, used:].astype(F32)
        lane = TILE * per * (rows // TILE)
        for t in range(bands):
            at = t // TILE * skip
            parts = [
                total[t % TILE : t % TILE + 1, at + i * 128 : at + (i + 1) * 128]
                for i in range(skip // 128)
            ]
            parts.append(jnp.zeros((TILE - skip // 128, 128), F32))
            out_ref[t, :, lane : lane + 128] = jnp.concatenate(parts, axis=0).astype(BF16)


def spectral_kernel(rows, tiles, has_piece, x_ref, filter_ref, table_ref, out_ref, *refs):
    x_all, out_all = refs[-2:]
    bands = x_ref.shape[0]
    blocks = rows // TILE
    stride = tiles * 128
    degrees = filter_ref.shape[1]
    half = table_ref.shape[0]
    if has_piece:
        total = x_ref[0, :, blocks * stride :].astype(F32)
        for t in range(1, bands):
            total = total + x_ref[t, :, blocks * stride :].astype(F32)
        refs[0][...] = total
    shape = (2 * TILE, degrees)
    odd = (lax.broadcasted_iota(jnp.int32, shape, 1) + lax.axis_index("lat")) % 2
    signs = (1 - 2 * odd).astype(F32)
    gains = jnp.concatenate([filter_ref[...], filter_ref[...]], axis=0)
    north = list(range(bands // 2))
    south = [bands - 1 - t for t in north]
    at = 0
    for g in range(tiles):
        depth = degrees - bands * TILE * g
        for h, order in enumerate((north, south)):
            parts = [
                x_ref[t, :, i * stride + g * 128 : i * stride + (g + 1) * 128].astype(F32)
                for t in order
                for i in range(blocks)
            ]
            place(x_all, jnp.concatenate(parts, axis=0).T, h * 128, 128)
        sign, gain = signs[:, degrees - depth :], gains[:, degrees - depth :]
        for r in range(TILE):
            starts = [h * 128 + 2 * r + p for h in range(2) for p in range(2)]
            modes = [pick(x_all, half, start, TILE, 2 * TILE) for start in starts]
            table = table_ref[:, at : at + depth]
            at += depth
            both = dot(jnp.concatenate(modes, axis=0).astype(BF16), table)
            spectrum = both[: 2 * TILE] + sign * both[2 * TILE :]
            filtered = spectrum * gain
            filtered = jnp.concatenate([filtered, sign * filtered], axis=0).astype(BF16)
            waves = dot(filtered, table, ((1,), (1,)))
            for i, start in enumerate(starts):
                place(out_all, waves[i * TILE : (i + 1) * TILE], start, TILE, 2 * TILE)
        for h, order in enumerate((north, south)):
            waves = pick(out_all, half, h * 128, 128).T.astype(BF16)
            for n, t in enumerate(order):
                for i in range(blocks):
                    lane = i * stride + g * 128
                    row = (n * blocks + i) * TILE
                    out_ref[t, :, lane : lane + 128] = waves[row : row + TILE]


def inverse_kernel(rows, cols, doubled, scaled, *refs):
    if scaled:
        x_ref, table_ref, scale_ref, piece_ref, out_ref, x_all = refs
    else:
        x_ref, table_ref, out_ref, x_all = refs
    bands = x_ref.shape[0]
    blocks = rows // TILE
    stride = x_ref.shape[2] // blocks
    share = 2 * TILE
    held = [
        [
            jnp.concatenate(
                [
                    x_ref[t, :, i * stride + g * 128 : i * stride + (g + 1) * 128].astype(F32)
                    for i in range(blocks)
                ],
                axis=0,
            )
            for g in range(stride // 128)
        ]
        for t in range(bands)
    ]
    for c in range(TILE):
        line = jnp.concatenate(
            [tile[:, c * share : (c + 1) * share] for one in held for tile in one], axis=1
        )
        place(x_all, line, c, rows, TILE)
    modes = table_ref.shape[0]
    x = pick(x_all, modes)
    if doubled:
        column = lax.broadcasted_iota(jnp.int32, x.shape, 1)
        x = x * jnp.where(column < 2, 1.0, 2.0)
    value = dot(x.astype(BF16), table_ref[...])
    chunks, _, lanes = out_ref.shape
    pad = lanes - rows * cols
    rest = jnp.zeros((TILE, pad), F32)
    if scaled:
        value = value * scale_ref[...]
        piece = piece_ref[...]
        rest = jnp.concatenate(
            [piece[i // 2 : i // 2 + 1, i % 2 * 64 : i % 2 * 64 + 64] for i in range(TILE)], axis=0
        )
    lines = [value[s * TILE : (s + 1) * TILE] for s in range(rows)]
    for b in range(chunks):
        parts = [line[:, b * cols : (b + 1) * cols] for line in lines]
        out_ref[b] = jnp.concatenate(parts + [rest], axis=1).astype(BF16)


def erf(values):
    return lax.erf(values)


def mlp_kernel(
    block, grad_scale,
    recv_ref, state_ref, cot_ref, up_ref, down_ref,
    send_ref, back_out,
    mixed, cots, active_all, back_pre_all, grads, back_ref, sem,
):
    rows, cols, channels = state_ref.shape
    chunks = recv_ref.shape[0]
    points = rows * cols
    mixed[...] = take_tile(recv_ref, points)
    for s in range(rows):
        at = pl.ds(s * cols, cols)
        row = slot_row(s, rows)
        mixed[at, :] = mixed[at, :] + state_ref[row].astype(F32)
        cots[at, :] = cot_ref[row].astype(F32)

    def step(index, _):
        at = pl.ds(pl.multiple_of(index * block, block), block)
        up = up_ref[...]
        pre = dot(mixed[at, :].astype(BF16), up)
        back_active = dot(cots[at, :].astype(BF16), down_ref[...])
        cdf = 0.5 * (1.0 + erf(pre * (1.0 / math.sqrt(2.0))))
        density = jnp.exp(-0.5 * pre * pre) * (1.0 / math.sqrt(2.0 * math.pi))
        active_all[at, :] = (pre * cdf).astype(BF16)
        back_pre = (back_active * (cdf + pre * density)).astype(BF16)
        back_pre_all[at, :] = back_pre
        back_ref[at, :] = cots[at, :] + dot(back_pre, up, ((1,), (1,)))
        return 0

    lax.fori_loop(0, points // block, step, 0)
    kept = pltpu.make_async_copy(back_ref, back_out, sem)
    kept.start()
    up_part = dot(mixed[...].astype(BF16), back_pre_all[...], ((0,), (0,)))
    down_part = dot(cots[...].astype(BF16), active_all[...], ((0,), (0,)))
    place(grads, up_part * grad_scale, lead=(0,))
    place(grads, down_part * grad_scale, lead=(1,))

    used = padded(points)
    per_band = chunks // 2
    bands = channels // per_band
    hidden = up_ref.shape[1]
    for b in range(chunks):
        line = pick(grads, hidden, b // 2, bands, per_band, lead=(b % 2,)).astype(BF16)
        for i in range(bands // TILE):
            send_ref[b, :, used + i * hidden : used + (i + 1) * hidden] = line[
                i * TILE : (i + 1) * TILE
            ]
    send_tile(send_ref, back_ref[...], used)
    kept.wait()


def join_kernel(recv_ref, back_ref, out_ref, up_ref, down_ref, held):
    rows, cols, _ = out_ref.shape
    points = rows * cols
    total = back_ref[...] + take_tile(recv_ref, points)
    for s in range(rows):
        out_ref[slot_row(s, rows)] = total[s * cols : (s + 1) * cols].astype(BF16)
    lines, hidden = up_ref.shape
    share = hidden // TILE
    for b in range(recv_ref.shape[0]):
        held[pl.ds(b * TILE, TILE), :] = jnp.concatenate(
            [recv_ref[b, :, points : points + share].astype(F32), jnp.zeros((TILE, 128 - share), F32)],
            axis=1,
        )
    for parity, ref in enumerate((up_ref, down_ref)):
        ref[...] = jnp.concatenate(
            [
                held[pl.ds(parity * TILE + i, lines, stride=2 * TILE), :][:, :share]
                for i in range(TILE)
            ],
            axis=1,
        )


def body(state_grid, spectral_filter, up_weight, down_weight, cotangent):
    _, rows, cols, channels = state_grid.shape
    bands, chunks = lax.axis_size("lat"), lax.axis_size("lon")
    band = lax.axis_index("lat")
    degrees = spectral_filter.shape[0]
    hidden = up_weight.shape[1]
    lat_total, lon_total = rows * bands, cols * chunks
    orders = degrees // bands
    points = rows * cols
    used = padded(points)
    modes = 2 * degrees
    line = TILE * 2 * orders
    wide = rows // TILE * line
    tiles = orders // TILE

    state = state_grid.reshape(rows, cols, channels)
    cot = cotangent.reshape(rows, cols, channels)

    sent = call(
        split_kernel,
        shaped((chunks, TILE, used), BF16),
        state,
        scratch=[pltpu.VMEM((points, channels), F32)],
    )
    whole = lax.all_to_all(sent, "lon", 0, 0, tiled=True)

    table, turned = fourier_tables(lon_total, bands, orders)
    legendre = legendre_tables(bands, orders, lat_total, degrees)
    gains = spectral_filter.T
    own = lax.dynamic_slice_in_dim(row_scale(lat_total, lon_total), band * rows, rows)
    own = jnp.where(band * 2 >= bands, jnp.flip(own), own)
    scale = jnp.repeat(own, TILE)[:, None]

    def forward(x, doubled, skip, *extra):
        return call(
            functools.partial(forward_kernel, rows, cols, doubled, bool(extra), skip),
            shaped((bands, TILE, wide + (128 if skip else 0)), BF16),
            x, table, *extra,
            scratch=[
                pltpu.VMEM((rows * TILE, lon_total), F32),
                tiles_of(rows * TILE, modes),
            ],
        )

    def turn(x):
        return lax.all_to_all(x, "lat", 0, 0, tiled=True)

    def spectral(x, has_piece):
        outs = [shaped((bands, TILE, wide), BF16)]
        if has_piece:
            outs.append(shaped((TILE, 128), F32))
        return call(
            functools.partial(spectral_kernel, rows, tiles, has_piece),
            outs,
            x, gains, legendre,
            scratch=[tiles_of(256, lat_total // 2)] * 2,
        )

    def inverse(x, doubled, *extra):
        return call(
            functools.partial(inverse_kernel, rows, cols, doubled, bool(extra)),
            shaped((chunks, TILE, used), BF16),
            x, turned, *extra,
            scratch=[tiles_of(rows * TILE, modes)],
        )

    spread = turn(forward(whole, False, 0, scale))
    waves = turn(spectral(spread, False)[0])
    smooth = lax.all_to_all(inverse(waves, True), "lon", 0, 0, tiled=True)

    sent, back_mixed = call(
        functools.partial(mlp_kernel, points // 6, 1.0 / math.sqrt(lat_total * lon_total)),
        [
            shaped((chunks, TILE, used + bands // TILE * hidden), BF16),
            shaped((points, channels), F32),
        ],
        smooth, state, cot, up_weight, down_weight,
        in_hbm=(1,),
        scratch=[
            pltpu.VMEM((points, channels), F32),
            pltpu.VMEM((points, channels), F32),
            pltpu.VMEM((points, hidden), BF16),
            pltpu.VMEM((points, hidden), BF16),
            pltpu.VMEM((2, hidden // 128, channels, 128), F32),
            pltpu.VMEM((points, channels), F32),
            pltpu.SemaphoreType.DMA,
        ],
    )
    whole = lax.all_to_all(sent, "lon", 0, 0, tiled=True)
    filtered, piece = spectral(turn(forward(whole, True, hidden)), True)
    back_waves = turn(filtered)
    field = lax.all_to_all(inverse(back_waves, False, scale, piece), "lon", 0, 0, tiled=True)
    grad_field, grad_up, grad_down = call(
        join_kernel,
        [
            shaped((rows, cols, channels), BF16),
            shaped((chunks // 2, hidden), F32),
            shaped((chunks // 2, hidden), F32),
        ],
        field, back_mixed,
        scratch=[pltpu.VMEM((chunks * TILE, 128), F32)],
    )
    return grad_field.reshape(state_grid.shape), grad_up, grad_down


def solution(mesh):
    placed = (P(None, "lat", "lon", None), P(None, "lon"), P(), P(), P(None, "lat", "lon", None))
    return jax.shard_map(
        body,
        mesh=mesh,
        in_specs=placed,
        out_specs=(P(None, "lat", "lon", None), P("lat", None), P("lat", None)),
        check_vma=False,
    )
```

```python
import functools
import math

import jax
import jax.numpy as jnp
from jax import lax
from jax.experimental import pallas as pl
from jax.experimental.pallas import tpu as pltpu
from jax.sharding import PartitionSpec as P

TILE = 8
F32 = jnp.float32
BF16 = jnp.bfloat16
VMEM_LIMIT = 24 * 1024 * 1024


def dot(a, b, dims=((1,), (0,))):
    return lax.dot_general(a, b, (dims, ((), ())), preferred_element_type=F32)


def call(kernel, outs, *args, scratch=(), cost=None, in_hbm=()):
    single = not isinstance(outs, (list, tuple))
    shapes = [outs] if single else list(outs)
    result = pl.pallas_call(
        kernel,
        out_shape=shapes,
        in_specs=[pl.BlockSpec(memory_space=pltpu.VMEM)] * len(args),
        out_specs=[
            pl.BlockSpec(memory_space=pltpu.HBM if i in in_hbm else pltpu.VMEM)
            for i in range(len(shapes))
        ],
        scratch_shapes=list(scratch),
        compiler_params=pltpu.CompilerParams(vmem_limit_bytes=VMEM_LIMIT),
        cost_estimate=cost,
    )(*args)
    return result[0] if single else result


def shaped(shape, dtype):
    return jax.ShapeDtypeStruct(shape, dtype)


def tiles_of(rows, width):
    return pltpu.VMEM((-(-width // 128), rows, 128), F32)


def pick(ref, width, start=0, size=None, stride=1, lead=()):
    tiles = -(-width // 128)
    at = slice(None) if size is None else pl.ds(start, size, stride=stride)
    value = jnp.concatenate([ref[(*lead, i, at, slice(None))] for i in range(tiles)], axis=1)
    return value[:, :width] if tiles * 128 > width else value


def place(ref, value, start=0, size=None, stride=1, lead=()):
    pad = -value.shape[1] % 128
    if pad:
        value = jnp.concatenate([value, jnp.zeros((value.shape[0], pad), value.dtype)], axis=1)
    at = slice(None) if size is None else pl.ds(start, size, stride=stride)
    for i in range(value.shape[1] // 128):
        ref[(*lead, i, at, slice(None))] = value[:, i * 128 : (i + 1) * 128]


def row_scale(lat_total, lon_total):
    colatitude = (jnp.arange(lat_total, dtype=F32) + 0.5) * (math.pi / lat_total)
    counter = jnp.arange(1, lat_total // 2 + 1, dtype=F32)
    series = jnp.sum(
        jnp.cos(2.0 * counter[None, :] * colatitude[:, None])
        / (4.0 * counter * counter - 1.0)[None, :],
        axis=1,
    )
    return 2.0 / lat_total * (1.0 - 2.0 * series) * (2.0 * math.pi / lon_total)


def wave_pair(product, lon_total):
    quarter = lon_total // 4
    turns = jnp.floor(product * (1.0 / quarter) + 0.5)
    angle = (product - turns * quarter) * (2.0 * math.pi / lon_total)
    square = angle * angle
    sine = angle * (
        1.0 + square * (-1.0 / 6 + square * (1.0 / 120 + square * (-1.0 / 5040 + square / 362880)))
    )
    cosine = 1.0 + square * (
        -0.5 + square * (1.0 / 24 + square * (-1.0 / 720 + square / 40320))
    )
    quadrant = turns - 4.0 * jnp.floor(turns * 0.25)
    odd = (quadrant == 1.0) | (quadrant == 3.0)
    first = jnp.where(odd, sine, cosine)
    second = jnp.where(odd, cosine, sine)
    first = jnp.where((quadrant == 1.0) | (quadrant == 2.0), -first, first)
    second = jnp.where(quadrant >= 2.0, -second, second)
    return first, second


def rotate(pair, turn):
    cosine, sine = pair
    turn_cos, turn_sin = turn
    return cosine * turn_cos - sine * turn_sin, sine * turn_cos + cosine * turn_sin


def phased(product, part, lon_total):
    cosine, sine = wave_pair(product, lon_total)
    return jnp.where(part == 1, -sine, cosine), jnp.where(part == 1, cosine, sine)


def fourier_kernel(bands, orders, start_ref, table_ref, turned_ref):
    lon_total, modes = table_ref.shape
    per = 2 * orders

    shape = (TILE, modes)
    column = lax.broadcasted_iota(jnp.int32, shape, 1)
    group = column // per
    rank = column - group * per
    order = (bands * (rank // 2) + group).astype(F32)
    row = lax.broadcasted_iota(jnp.int32, shape, 0).astype(F32)
    turn = wave_pair(TILE * order, lon_total)

    def step(index, pair):
        later = rotate(pair, turn)
        at = pl.ds(pl.multiple_of(index * 2 * TILE, 2 * TILE), 2 * TILE)
        table_ref[at, :] = jnp.concatenate([pair[0], later[0]], axis=0).astype(BF16)
        return rotate(later, turn)

    lax.fori_loop(0, lon_total // (2 * TILE), step, phased(row * order, rank % 2, lon_total))

    shape = (TILE, lon_total)
    lon_index = lax.broadcasted_iota(jnp.int32, shape, 1).astype(F32)
    row = lax.broadcasted_iota(jnp.int32, shape, 0)
    start = phased((bands * (row // 2)).astype(F32) * lon_index, row % 2, lon_total)
    inner = wave_pair(TILE // 2 * bands * lon_index, lon_total)
    outer = wave_pair(lon_index, lon_total)

    def group_step(t, pair):
        now = pair
        for i in range(per // (2 * TILE)):
            later = rotate(now, inner)
            at = pl.ds(pl.multiple_of(t * per + i * 2 * TILE, 2 * TILE), 2 * TILE)
            turned_ref[at, :] = jnp.concatenate([now[0], later[0]], axis=0).astype(BF16)
            now = rotate(later, inner)
        return rotate(pair, outer)

    lax.fori_loop(0, modes // per, group_step, start)


def fourier_tables(start, lon_total, bands, orders):
    modes = 2 * bands * orders
    shapes = [(lon_total, modes), (modes, lon_total)]
    return call(
        functools.partial(fourier_kernel, bands, orders),
        [shaped(shape, BF16) for shape in shapes],
        start,
        cost=pl.CostEstimate(
            flops=30 * modes * lon_total, bytes_accessed=8 * modes * lon_total, transcendentals=0
        ),
    )


def legendre_kernel(bands, degrees, cos_ref, diag_ref, out_ref, *tables):
    tiles = diag_ref.shape[0] // TILE
    band = lax.axis_index("lat")
    cosine = cos_ref[...]
    width = cosine.shape[1]
    shape = (TILE, 128)
    rank = lax.broadcasted_iota(jnp.int32, shape, 0)
    orders = [(bands * (TILE * g + rank) + band).astype(F32) for g in range(tiles)]
    diags = [diag_ref[g * TILE : (g + 1) * TILE, :] for g in range(tiles)]

    def spread(value):
        return jnp.concatenate([value] * (-(-width // 128)), axis=1)[:, :width]

    def block(active, index, carry):
        carry = list(carry)
        for g in range(active):
            here, before, scale, inverse = carry[g]
            order = orders[g]
            square = order * order
            wide_order = spread(order)
            level = jnp.exp(diags[g] + scale)
            for inner in range(TILE):
                degree = index * TILE + inner
                lv = jnp.full(shape, degree, jnp.int32).astype(F32)
                now = jnp.sqrt(jnp.maximum(lv * lv - square, 0.0) / jnp.maximum(4.0 * lv * lv - 1.0, 1.0))
                live = lv > order
                growth = 1.0 / jnp.where(live, now, 1.0)
                ahead = spread(growth) * cosine * here - spread(growth * inverse) * before
                wide_live = spread(lv) > wide_order
                here, before = jnp.where(wide_live, ahead, here), jnp.where(wide_live, here, before)
                values = jnp.where(spread(lv) >= wide_order, level * here, 0.0)
                at = pl.multiple_of((degree - bands * TILE * g) * TILE, TILE)
                place(tables[g], values, at, TILE)
                inverse = now
            largest = jnp.maximum(jnp.abs(here), jnp.abs(before))
            carry[g] = (here / largest, before / largest, scale + jnp.log(largest), inverse)
        return tuple(carry)

    ones = jnp.ones((TILE, width), F32)
    zeros = jnp.zeros((TILE, width), F32)
    carry = tuple((ones, zeros, zeros, jnp.zeros(shape, F32)) for _ in range(tiles))
    for g in range(tiles):
        last = bands * (g + 1) if g + 1 < tiles else degrees // TILE
        carry = lax.fori_loop(bands * g, last, functools.partial(block, g + 1), carry)
    at = 0
    for g in range(tiles):
        depth = degrees - bands * TILE * g
        for r in range(TILE):
            rows = pick(tables[g], width, r, depth, TILE)
            out_ref[:, at : at + depth] = rows.T.astype(BF16)
            at += depth


def legendre_tables(bands, orders, lat_total, degrees):
    half = lat_total // 2
    colatitude = (jnp.arange(half, dtype=F32) + 0.5) * (math.pi / lat_total)
    cosine = jnp.cos(colatitude)
    log_sine = jnp.log(jnp.sin(colatitude))
    later = jnp.arange(1, degrees, dtype=F32)
    ratios = jnp.log((2.0 * later - 1.0) / (2.0 * later))
    order = (bands * jnp.arange(orders, dtype=jnp.int32) + lax.axis_index("lat")).astype(F32)
    partial_logs = jnp.sum(jnp.where(later[None, :] <= order[:, None], ratios[None, :], 0.0), axis=1)
    base_logs = 0.5 * (jnp.log((2.0 * order + 1.0) / (4.0 * math.pi)) + partial_logs)
    diag = base_logs[:, None] + order[:, None] * log_sine[None, :]
    depths = [degrees - bands * TILE * g for g in range(orders // TILE)]
    return call(
        functools.partial(legendre_kernel, bands, degrees),
        shaped((half, TILE * sum(depths)), BF16),
        jnp.broadcast_to(cosine[None, :], (TILE, half)),
        diag,
        scratch=[tiles_of(depth * TILE, half) for depth in depths],
        cost=pl.CostEstimate(flops=40_000_000, bytes_accessed=6_000_000, transcendentals=1_000_000),
    )


def slot_row(slot, rows):
    south = lax.axis_index("lat") * 2 >= lax.axis_size("lat")
    return jnp.where(south, rows - 1 - slot, slot)


def padded(count):
    return -(-count // 128) * 128


def send_tile(ref, grid, used):
    turned = grid.T
    pad = used - turned.shape[1]
    if pad:
        turned = jnp.concatenate([turned, jnp.zeros((turned.shape[0], pad), F32)], axis=1)
    for b in range(ref.shape[0]):
        ref[b, :, :used] = turned[b * TILE : (b + 1) * TILE].astype(BF16)


def take_tile(ref, points):
    chunks = [ref[b].astype(F32) for b in range(ref.shape[0])]
    return jnp.concatenate(chunks, axis=0).T[:points]


def split_kernel(x_ref, out_ref, grid):
    rows, cols, _ = x_ref.shape
    for s in range(rows):
        grid[pl.ds(s * cols, cols), :] = x_ref[slot_row(s, rows)].astype(F32)
    send_tile(out_ref, grid[...], out_ref.shape[2])


def forward_kernel(rows, cols, doubled, scaled, skip, *refs):
    if scaled:
        x_ref, table_ref, scale_ref, out_ref, x_all, out_all = refs
    else:
        x_ref, table_ref, out_ref, x_all, out_all = refs
    chunks = x_ref.shape[0]
    used = padded(rows * cols)
    held = [x_ref[b, :, :used].astype(F32) for b in range(chunks)]
    for s in range(rows):
        x_all[pl.ds(s * TILE, TILE), :] = jnp.concatenate(
            [one[:, s * cols : (s + 1) * cols] for one in held], axis=1
        )
    value = dot(x_all[...].astype(BF16), table_ref[...])
    if scaled:
        value = value * scale_ref[...]
    if doubled:
        column = lax.broadcasted_iota(jnp.int32, value.shape, 1)
        value = value * jnp.where(column < 2, 1.0, 2.0)
    modes = value.shape[1]
    place(out_all, value)
    lines = [pick(out_all, modes, c, rows, TILE) for c in range(TILE)]
    bands = out_ref.shape[0]
    per = modes // bands
    share = 2 * TILE
    for t in range(bands):
        for g in range(per // share):
            at = t * per + g * share
            tile = jnp.concatenate([line[:, at : at + share] for line in lines], axis=1).astype(BF16)
            for i in range(rows // TILE):
                lane = i * TILE * per + g * 128
                out_ref[t, :, lane : lane + 128] = tile[i * TILE : (i + 1) * TILE]
    if skip:
        total = x_ref[0, :, used:].astype(F32)
        for b in range(1, chunks):
            total = total + x_ref[b, :, used:].astype(F32)
        lane = TILE * per * (rows // TILE)
        for t in range(bands):
            at = t // TILE * skip
            parts = [
                total[t % TILE : t % TILE + 1, at + i * 128 : at + (i + 1) * 128]
                for i in range(skip // 128)
            ]
            parts.append(jnp.zeros((TILE - skip // 128, 128), F32))
            out_ref[t, :, lane : lane + 128] = jnp.concatenate(parts, axis=0).astype(BF16)


def spectral_kernel(rows, tiles, has_piece, x_ref, filter_ref, table_ref, out_ref, *refs):
    x_all, out_all = refs[-2:]
    bands = x_ref.shape[0]
    blocks = rows // TILE
    stride = tiles * 128
    degrees = filter_ref.shape[1]
    half = table_ref.shape[0]
    if has_piece:
        total = x_ref[0, :, blocks * stride :].astype(F32)
        for t in range(1, bands):
            total = total + x_ref[t, :, blocks * stride :].astype(F32)
        refs[0][...] = total
    shape = (2 * TILE, degrees)
    odd = (lax.broadcasted_iota(jnp.int32, shape, 1) + lax.axis_index("lat")) % 2
    signs = (1 - 2 * odd).astype(F32)
    gains = jnp.concatenate([filter_ref[...], filter_ref[...]], axis=0)
    north = list(range(bands // 2))
    south = [bands - 1 - t for t in north]
    at = 0
    for g in range(tiles):
        depth = degrees - bands * TILE * g
        for h, order in enumerate((north, south)):
            parts = [
                x_ref[t, :, i * stride + g * 128 : i * stride + (g + 1) * 128].astype(F32)
                for t in order
                for i in range(blocks)
            ]
            place(x_all, jnp.concatenate(parts, axis=0).T, h * 128, 128)
        sign, gain = signs[:, degrees - depth :], gains[:, degrees - depth :]
        for r in range(TILE):
            starts = [h * 128 + 2 * r + p for h in range(2) for p in range(2)]
            modes = [pick(x_all, half, start, TILE, 2 * TILE) for start in starts]
            table = table_ref[:, at : at + depth]
            at += depth
            both = dot(jnp.concatenate(modes, axis=0).astype(BF16), table)
            spectrum = both[: 2 * TILE] + sign * both[2 * TILE :]
            filtered = spectrum * gain
            filtered = jnp.concatenate([filtered, sign * filtered], axis=0).astype(BF16)
            waves = dot(filtered, table, ((1,), (1,)))
            for i, start in enumerate(starts):
                place(out_all, waves[i * TILE : (i + 1) * TILE], start, TILE, 2 * TILE)
        for h, order in enumerate((north, south)):
            waves = pick(out_all, half, h * 128, 128).T.astype(BF16)
            for n, t in enumerate(order):
                for i in range(blocks):
                    lane = i * stride + g * 128
                    row = (n * blocks + i) * TILE
                    out_ref[t, :, lane : lane + 128] = waves[row : row + TILE]


def inverse_kernel(rows, cols, doubled, scaled, *refs):
    if scaled:
        x_ref, table_ref, scale_ref, piece_ref, out_ref, x_all = refs
    else:
        x_ref, table_ref, out_ref, x_all = refs
    bands = x_ref.shape[0]
    blocks = rows // TILE
    stride = x_ref.shape[2] // blocks
    share = 2 * TILE
    held = [
        [
            jnp.concatenate(
                [
                    x_ref[t, :, i * stride + g * 128 : i * stride + (g + 1) * 128].astype(F32)
                    for i in range(blocks)
                ],
                axis=0,
            )
            for g in range(stride // 128)
        ]
        for t in range(bands)
    ]
    for c in range(TILE):
        line = jnp.concatenate(
            [tile[:, c * share : (c + 1) * share] for one in held for tile in one], axis=1
        )
        place(x_all, line, c, rows, TILE)
    modes = table_ref.shape[0]
    x = pick(x_all, modes)
    if doubled:
        column = lax.broadcasted_iota(jnp.int32, x.shape, 1)
        x = x * jnp.where(column < 2, 1.0, 2.0)
    value = dot(x.astype(BF16), table_ref[...])
    chunks, _, lanes = out_ref.shape
    pad = lanes - rows * cols
    rest = jnp.zeros((TILE, pad), F32)
    if scaled:
        value = value * scale_ref[...]
        piece = piece_ref[...]
        rest = jnp.concatenate(
            [piece[i // 2 : i // 2 + 1, i % 2 * 64 : i % 2 * 64 + 64] for i in range(TILE)], axis=0
        )
    lines = [value[s * TILE : (s + 1) * TILE] for s in range(rows)]
    for b in range(chunks):
        parts = [line[:, b * cols : (b + 1) * cols] for line in lines]
        out_ref[b] = jnp.concatenate(parts + [rest], axis=1).astype(BF16)


def mlp_kernel(
    grad_scale,
    recv_ref, state_ref, cot_ref, up_ref, down_ref,
    send_ref, back_out,
    mixed, cots, active_all, back_pre_all, grads, back_ref, sem,
):
    rows, cols, channels = state_ref.shape
    chunks = recv_ref.shape[0]
    points = rows * cols
    mixed[...] = take_tile(recv_ref, points)
    for s in range(rows):
        at = pl.ds(s * cols, cols)
        row = slot_row(s, rows)
        mixed[at, :] = mixed[at, :] + state_ref[row].astype(F32)
        cots[at, :] = cot_ref[row].astype(F32)

    up = up_ref[...]
    mixed_low = mixed[...].astype(BF16)
    cot_low = cots[...].astype(BF16)
    pre = dot(mixed_low, up)
    back_active = dot(cot_low, down_ref[...])
    cdf = 0.5 * (1.0 + lax.erf(pre * (1.0 / math.sqrt(2.0))))
    density = jnp.exp(-0.5 * pre * pre) * (1.0 / math.sqrt(2.0 * math.pi))
    active_all[...] = (pre * cdf).astype(BF16)
    back_pre_all[...] = (back_active * (cdf + pre * density)).astype(BF16)
    back_ref[...] = cots[...] + dot(back_pre_all[...], up, ((1,), (1,)))
    kept = pltpu.make_async_copy(back_ref, back_out, sem)
    kept.start()
    up_part = dot(mixed_low, back_pre_all[...], ((0,), (0,)))
    down_part = dot(cot_low, active_all[...], ((0,), (0,)))
    place(grads, up_part * grad_scale, lead=(0,))
    place(grads, down_part * grad_scale, lead=(1,))

    used = padded(points)
    per_band = chunks // 2
    bands = channels // per_band
    hidden = up_ref.shape[1]
    for b in range(chunks):
        line = pick(grads, hidden, b // 2, bands, per_band, lead=(b % 2,)).astype(BF16)
        for i in range(bands // TILE):
            send_ref[b, :, used + i * hidden : used + (i + 1) * hidden] = line[
                i * TILE : (i + 1) * TILE
            ]
    send_tile(send_ref, back_ref[...], used)
    kept.wait()


def join_kernel(recv_ref, back_ref, out_ref, up_ref, down_ref, held):
    rows, cols, _ = out_ref.shape
    points = rows * cols
    total = back_ref[...] + take_tile(recv_ref, points)
    for s in range(rows):
        out_ref[slot_row(s, rows)] = total[s * cols : (s + 1) * cols].astype(BF16)
    lines, hidden = up_ref.shape
    share = hidden // TILE
    for b in range(recv_ref.shape[0]):
        held[pl.ds(b * TILE, TILE), :] = jnp.concatenate(
            [recv_ref[b, :, points : points + share].astype(F32), jnp.zeros((TILE, 128 - share), F32)],
            axis=1,
        )
    for parity, ref in enumerate((up_ref, down_ref)):
        ref[...] = jnp.concatenate(
            [
                held[pl.ds(parity * TILE + i, lines, stride=2 * TILE), :][:, :share]
                for i in range(TILE)
            ],
            axis=1,
        )


def body(state_grid, spectral_filter, up_weight, down_weight, cotangent):
    _, rows, cols, channels = state_grid.shape
    bands, chunks = lax.axis_size("lat"), lax.axis_size("lon")
    band = lax.axis_index("lat")
    degrees = spectral_filter.shape[0]
    hidden = up_weight.shape[1]
    lat_total, lon_total = rows * bands, cols * chunks
    orders = degrees // bands
    points = rows * cols
    used = padded(points)
    modes = 2 * degrees
    line = TILE * 2 * orders
    wide = rows // TILE * line
    tiles = orders // TILE

    state = state_grid.reshape(rows, cols, channels)
    cot = cotangent.reshape(rows, cols, channels)

    sent = call(
        split_kernel,
        shaped((chunks, TILE, used), BF16),
        state,
        scratch=[pltpu.VMEM((points, channels), F32)],
    )
    whole = lax.all_to_all(sent, "lon", 0, 0, tiled=True)

    legendre = legendre_tables(bands, orders, lat_total, degrees)
    start, legendre = lax.optimization_barrier((jnp.zeros((TILE, 128), F32), legendre))
    table, turned = fourier_tables(start, lon_total, bands, orders)
    gains = spectral_filter.T
    own = lax.dynamic_slice_in_dim(row_scale(lat_total, lon_total), band * rows, rows)
    own = jnp.where(band * 2 >= bands, jnp.flip(own), own)
    scale = jnp.repeat(own, TILE)[:, None]

    def forward(x, doubled, skip, *extra):
        return call(
            functools.partial(forward_kernel, rows, cols, doubled, bool(extra), skip),
            shaped((bands, TILE, wide + (128 if skip else 0)), BF16),
            x, table, *extra,
            scratch=[
                pltpu.VMEM((rows * TILE, lon_total), F32),
                tiles_of(rows * TILE, modes),
            ],
        )

    def turn(x):
        return lax.all_to_all(x, "lat", 0, 0, tiled=True)

    def spectral(x, has_piece):
        outs = [shaped((bands, TILE, wide), BF16)]
        if has_piece:
            outs.append(shaped((TILE, 128), F32))
        return call(
            functools.partial(spectral_kernel, rows, tiles, has_piece),
            outs,
            x, gains, legendre,
            scratch=[tiles_of(256, lat_total // 2)] * 2,
        )

    def inverse(x, doubled, *extra):
        return call(
            functools.partial(inverse_kernel, rows, cols, doubled, bool(extra)),
            shaped((chunks, TILE, used), BF16),
            x, turned, *extra,
            scratch=[tiles_of(rows * TILE, modes)],
        )

    spread = turn(forward(whole, False, 0, scale))
    waves = turn(spectral(spread, False)[0])
    smooth = lax.all_to_all(inverse(waves, True), "lon", 0, 0, tiled=True)

    sent, back_mixed = call(
        functools.partial(mlp_kernel, 1.0 / math.sqrt(lat_total * lon_total)),
        [
            shaped((chunks, TILE, used + bands // TILE * hidden), BF16),
            shaped((points, channels), F32),
        ],
        smooth, state, cot, up_weight, down_weight,
        in_hbm=(1,),
        scratch=[
            pltpu.VMEM((points, channels), F32),
            pltpu.VMEM((points, channels), F32),
            pltpu.VMEM((points, hidden), BF16),
            pltpu.VMEM((points, hidden), BF16),
            pltpu.VMEM((2, hidden // 128, channels, 128), F32),
            pltpu.VMEM((points, channels), F32),
            pltpu.SemaphoreType.DMA,
        ],
    )
    whole = lax.all_to_all(sent, "lon", 0, 0, tiled=True)
    filtered, piece = spectral(turn(forward(whole, True, hidden)), True)
    back_waves = turn(filtered)
    field = lax.all_to_all(inverse(back_waves, False, scale, piece), "lon", 0, 0, tiled=True)
    grad_field, grad_up, grad_down = call(
        join_kernel,
        [
            shaped((rows, cols, channels), BF16),
            shaped((chunks // 2, hidden), F32),
            shaped((chunks // 2, hidden), F32),
        ],
        field, back_mixed,
        scratch=[pltpu.VMEM((chunks * TILE, 128), F32)],
    )
    return grad_field.reshape(state_grid.shape), grad_up, grad_down


def solution(mesh):
    placed = (P(None, "lat", "lon", None), P(None, "lon"), P(), P(), P(None, "lat", "lon", None))
    return jax.shard_map(
        body,
        mesh=mesh,
        in_specs=placed,
        out_specs=(P(None, "lat", "lon", None), P("lat", None), P("lat", None)),
        check_vma=False,
    )
```

```python
import functools
import math

import jax
import jax.numpy as jnp
from jax import lax
from jax.experimental import pallas as pl
from jax.experimental.pallas import tpu as pltpu
from jax.sharding import PartitionSpec as P

TILE = 8
F32 = jnp.float32
BF16 = jnp.bfloat16
VMEM_LIMIT = 24 * 1024 * 1024


def dot(a, b, dims=((1,), (0,))):
    return lax.dot_general(a, b, (dims, ((), ())), preferred_element_type=F32)


def call(kernel, outs, *args, scratch=(), cost=None, in_hbm=()):
    single = not isinstance(outs, (list, tuple))
    shapes = [outs] if single else list(outs)
    result = pl.pallas_call(
        kernel,
        out_shape=shapes,
        in_specs=[pl.BlockSpec(memory_space=pltpu.VMEM)] * len(args),
        out_specs=[
            pl.BlockSpec(memory_space=pltpu.HBM if i in in_hbm else pltpu.VMEM)
            for i in range(len(shapes))
        ],
        scratch_shapes=list(scratch),
        compiler_params=pltpu.CompilerParams(vmem_limit_bytes=VMEM_LIMIT),
        cost_estimate=cost,
    )(*args)
    return result[0] if single else result


def shaped(shape, dtype):
    return jax.ShapeDtypeStruct(shape, dtype)


def tiles_of(rows, width):
    return pltpu.VMEM((-(-width // 128), rows, 128), F32)


def pick(ref, width, start=0, size=None, stride=1, lead=()):
    tiles = -(-width // 128)
    at = slice(None) if size is None else pl.ds(start, size, stride=stride)
    value = jnp.concatenate([ref[(*lead, i, at, slice(None))] for i in range(tiles)], axis=1)
    return value[:, :width] if tiles * 128 > width else value


def place(ref, value, start=0, size=None, stride=1, lead=()):
    pad = -value.shape[1] % 128
    if pad:
        value = jnp.concatenate([value, jnp.zeros((value.shape[0], pad), value.dtype)], axis=1)
    at = slice(None) if size is None else pl.ds(start, size, stride=stride)
    for i in range(value.shape[1] // 128):
        ref[(*lead, i, at, slice(None))] = value[:, i * 128 : (i + 1) * 128]


def row_scale(lat_total, lon_total):
    colatitude = (jnp.arange(lat_total, dtype=F32) + 0.5) * (math.pi / lat_total)
    counter = jnp.arange(1, lat_total // 2 + 1, dtype=F32)
    series = jnp.sum(
        jnp.cos(2.0 * counter[None, :] * colatitude[:, None])
        / (4.0 * counter * counter - 1.0)[None, :],
        axis=1,
    )
    return 2.0 / lat_total * (1.0 - 2.0 * series) * (2.0 * math.pi / lon_total)


def wave_pair(product, lon_total):
    quarter = lon_total // 4
    turns = jnp.floor(product * (1.0 / quarter) + 0.5)
    angle = (product - turns * quarter) * (2.0 * math.pi / lon_total)
    square = angle * angle
    sine = angle * (
        1.0 + square * (-1.0 / 6 + square * (1.0 / 120 + square * (-1.0 / 5040 + square / 362880)))
    )
    cosine = 1.0 + square * (
        -0.5 + square * (1.0 / 24 + square * (-1.0 / 720 + square / 40320))
    )
    quadrant = turns - 4.0 * jnp.floor(turns * 0.25)
    odd = (quadrant == 1.0) | (quadrant == 3.0)
    first = jnp.where(odd, sine, cosine)
    second = jnp.where(odd, cosine, sine)
    first = jnp.where((quadrant == 1.0) | (quadrant == 2.0), -first, first)
    second = jnp.where(quadrant >= 2.0, -second, second)
    return first, second


def rotate(pair, turn):
    cosine, sine = pair
    turn_cos, turn_sin = turn
    return cosine * turn_cos - sine * turn_sin, sine * turn_cos + cosine * turn_sin


def phased(product, part, lon_total):
    cosine, sine = wave_pair(product, lon_total)
    return jnp.where(part == 1, -sine, cosine), jnp.where(part == 1, cosine, sine)


def fourier_kernel(bands, orders, table_out, turned_out, table_ref, turned_ref, sems):
    lon_total, modes = table_ref.shape
    per = 2 * orders

    shape = (TILE, modes)
    column = lax.broadcasted_iota(jnp.int32, shape, 1)
    group = column // per
    rank = column - group * per
    order = (bands * (rank // 2) + group).astype(F32)
    row = lax.broadcasted_iota(jnp.int32, shape, 0).astype(F32)
    turn = wave_pair(TILE * order, lon_total)

    def step(index, pair):
        later = rotate(pair, turn)
        at = pl.ds(pl.multiple_of(index * 2 * TILE, 2 * TILE), 2 * TILE)
        table_ref[at, :] = jnp.concatenate([pair[0], later[0]], axis=0).astype(BF16)
        return rotate(later, turn)

    lax.fori_loop(0, lon_total // (2 * TILE), step, phased(row * order, rank % 2, lon_total))
    first = pltpu.make_async_copy(table_ref, table_out, sems.at[0])
    first.start()

    shape = (TILE, lon_total)
    lon_index = lax.broadcasted_iota(jnp.int32, shape, 1).astype(F32)
    row = lax.broadcasted_iota(jnp.int32, shape, 0)
    start = phased((bands * (row // 2)).astype(F32) * lon_index, row % 2, lon_total)
    inner = wave_pair(TILE // 2 * bands * lon_index, lon_total)
    outer = wave_pair(lon_index, lon_total)

    def group_step(t, pair):
        now = pair
        for i in range(per // (2 * TILE)):
            later = rotate(now, inner)
            at = pl.ds(pl.multiple_of(t * per + i * 2 * TILE, 2 * TILE), 2 * TILE)
            turned_ref[at, :] = jnp.concatenate([now[0], later[0]], axis=0).astype(BF16)
            now = rotate(later, inner)
        return rotate(pair, outer)

    lax.fori_loop(0, modes // per, group_step, start)
    second = pltpu.make_async_copy(turned_ref, turned_out, sems.at[1])
    second.start()
    first.wait()
    second.wait()


def fourier_tables(lon_total, bands, orders):
    modes = 2 * bands * orders
    shapes = [(lon_total, modes), (modes, lon_total)]
    return call(
        functools.partial(fourier_kernel, bands, orders),
        [shaped(shape, BF16) for shape in shapes],
        scratch=[pltpu.VMEM(shape, BF16) for shape in shapes] + [pltpu.SemaphoreType.DMA((2,))],
        cost=pl.CostEstimate(
            flops=30 * modes * lon_total, bytes_accessed=8 * modes * lon_total, transcendentals=0
        ),
        in_hbm=(0, 1),
    )


def legendre_kernel(bands, degrees, cos_ref, diag_ref, out_ref, *tables):
    tiles = diag_ref.shape[0] // TILE
    band = lax.axis_index("lat")
    cosine = cos_ref[...]
    width = cosine.shape[1]
    shape = (TILE, 128)
    rank = lax.broadcasted_iota(jnp.int32, shape, 0)
    orders = [(bands * (TILE * g + rank) + band).astype(F32) for g in range(tiles)]
    diags = [diag_ref[g * TILE : (g + 1) * TILE, :] for g in range(tiles)]

    def spread(value):
        return jnp.concatenate([value] * (-(-width // 128)), axis=1)[:, :width]

    def block(active, index, carry):
        carry = list(carry)
        for g in range(active):
            here, before, scale, inverse = carry[g]
            order = orders[g]
            square = order * order
            wide_order = spread(order)
            level = jnp.exp(diags[g] + scale)
            for inner in range(TILE):
                degree = index * TILE + inner
                lv = jnp.full(shape, degree, jnp.int32).astype(F32)
                now = jnp.sqrt(jnp.maximum(lv * lv - square, 0.0) / jnp.maximum(4.0 * lv * lv - 1.0, 1.0))
                live = lv > order
                growth = 1.0 / jnp.where(live, now, 1.0)
                ahead = spread(growth) * cosine * here - spread(growth * inverse) * before
                wide_live = spread(lv) > wide_order
                here, before = jnp.where(wide_live, ahead, here), jnp.where(wide_live, here, before)
                values = jnp.where(spread(lv) >= wide_order, level * here, 0.0)
                at = pl.multiple_of((degree - bands * TILE * g) * TILE, TILE)
                place(tables[g], values, at, TILE)
                inverse = now
            largest = jnp.maximum(jnp.abs(here), jnp.abs(before))
            carry[g] = (here / largest, before / largest, scale + jnp.log(largest), inverse)
        return tuple(carry)

    ones = jnp.ones((TILE, width), F32)
    zeros = jnp.zeros((TILE, width), F32)
    carry = tuple((ones, zeros, zeros, jnp.zeros(shape, F32)) for _ in range(tiles))
    for g in range(tiles):
        last = bands * (g + 1) if g + 1 < tiles else degrees // TILE
        carry = lax.fori_loop(bands * g, last, functools.partial(block, g + 1), carry)
    at = 0
    for g in range(tiles):
        depth = degrees - bands * TILE * g
        for r in range(TILE):
            rows = pick(tables[g], width, r, depth, TILE)
            out_ref[:, at : at + depth] = rows.T.astype(BF16)
            at += depth


def legendre_tables(bands, orders, lat_total, degrees):
    half = lat_total // 2
    colatitude = (jnp.arange(half, dtype=F32) + 0.5) * (math.pi / lat_total)
    cosine = jnp.cos(colatitude)
    log_sine = jnp.log(jnp.sin(colatitude))
    later = jnp.arange(1, degrees, dtype=F32)
    ratios = jnp.log((2.0 * later - 1.0) / (2.0 * later))
    order = (bands * jnp.arange(orders, dtype=jnp.int32) + lax.axis_index("lat")).astype(F32)
    partial_logs = jnp.sum(jnp.where(later[None, :] <= order[:, None], ratios[None, :], 0.0), axis=1)
    base_logs = 0.5 * (jnp.log((2.0 * order + 1.0) / (4.0 * math.pi)) + partial_logs)
    diag = base_logs[:, None] + order[:, None] * log_sine[None, :]
    depths = [degrees - bands * TILE * g for g in range(orders // TILE)]
    return call(
        functools.partial(legendre_kernel, bands, degrees),
        shaped((half, TILE * sum(depths)), BF16),
        jnp.broadcast_to(cosine[None, :], (TILE, half)),
        diag,
        scratch=[tiles_of(depth * TILE, half) for depth in depths],
        cost=pl.CostEstimate(flops=40_000_000, bytes_accessed=6_000_000, transcendentals=1_000_000),
    )


def slot_row(slot, rows):
    south = lax.axis_index("lat") * 2 >= lax.axis_size("lat")
    return jnp.where(south, rows - 1 - slot, slot)


def padded(count):
    return -(-count // 128) * 128


def send_tile(ref, grid, used):
    turned = grid.T
    pad = used - turned.shape[1]
    if pad:
        turned = jnp.concatenate([turned, jnp.zeros((turned.shape[0], pad), F32)], axis=1)
    for b in range(ref.shape[0]):
        ref[b, :, :used] = turned[b * TILE : (b + 1) * TILE].astype(BF16)


def take_tile(ref, points):
    chunks = [ref[b].astype(F32) for b in range(ref.shape[0])]
    return jnp.concatenate(chunks, axis=0).T[:points]


def split_kernel(x_ref, out_ref, grid):
    rows, cols, _ = x_ref.shape
    for s in range(rows):
        grid[pl.ds(s * cols, cols), :] = x_ref[slot_row(s, rows)].astype(F32)
    send_tile(out_ref, grid[...], out_ref.shape[2])


def forward_kernel(rows, cols, doubled, scaled, skip, *refs):
    if scaled:
        x_ref, table_ref, scale_ref, out_ref, x_all, out_all = refs
    else:
        x_ref, table_ref, out_ref, x_all, out_all = refs
    chunks = x_ref.shape[0]
    used = padded(rows * cols)
    held = [x_ref[b, :, :used].astype(F32) for b in range(chunks)]
    for s in range(rows):
        x_all[pl.ds(s * TILE, TILE), :] = jnp.concatenate(
            [one[:, s * cols : (s + 1) * cols] for one in held], axis=1
        )
    value = dot(x_all[...].astype(BF16), table_ref[...])
    if scaled:
        value = value * scale_ref[...]
    if doubled:
        column = lax.broadcasted_iota(jnp.int32, value.shape, 1)
        value = value * jnp.where(column < 2, 1.0, 2.0)
    modes = value.shape[1]
    place(out_all, value)
    lines = [pick(out_all, modes, c, rows, TILE) for c in range(TILE)]
    bands = out_ref.shape[0]
    per = modes // bands
    share = 2 * TILE
    for t in range(bands):
        for g in range(per // share):
            at = t * per + g * share
            tile = jnp.concatenate([line[:, at : at + share] for line in lines], axis=1).astype(BF16)
            for i in range(rows // TILE):
                lane = i * TILE * per + g * 128
                out_ref[t, :, lane : lane + 128] = tile[i * TILE : (i + 1) * TILE]
    if skip:
        total = x_ref[0, :, used:].astype(F32)
        for b in range(1, chunks):
            total = total + x_ref[b, :, used:].astype(F32)
        lane = TILE * per * (rows // TILE)
        for t in range(bands):
            at = t // TILE * skip
            parts = [
                total[t % TILE : t % TILE + 1, at + i * 128 : at + (i + 1) * 128]
                for i in range(skip // 128)
            ]
            parts.append(jnp.zeros((TILE - skip // 128, 128), F32))
            out_ref[t, :, lane : lane + 128] = jnp.concatenate(parts, axis=0).astype(BF16)


def spectral_kernel(rows, tiles, has_piece, x_ref, filter_ref, table_ref, out_ref, *refs):
    x_all, out_all = refs[-2:]
    bands = x_ref.shape[0]
    blocks = rows // TILE
    stride = tiles * 128
    degrees = filter_ref.shape[1]
    half = table_ref.shape[0]
    if has_piece:
        total = x_ref[0, :, blocks * stride :].astype(F32)
        for t in range(1, bands):
            total = total + x_ref[t, :, blocks * stride :].astype(F32)
        refs[0][...] = total
    shape = (2 * TILE, degrees)
    odd = (lax.broadcasted_iota(jnp.int32, shape, 1) + lax.axis_index("lat")) % 2
    signs = (1 - 2 * odd).astype(F32)
    gains = jnp.concatenate([filter_ref[...], filter_ref[...]], axis=0)
    north = list(range(bands // 2))
    south = [bands - 1 - t for t in north]
    at = 0
    for g in range(tiles):
        depth = degrees - bands * TILE * g
        for h, order in enumerate((north, south)):
            parts = [
                x_ref[t, :, i * stride + g * 128 : i * stride + (g + 1) * 128].astype(F32)
                for t in order
                for i in range(blocks)
            ]
            place(x_all, jnp.concatenate(parts, axis=0).T, h * 128, 128)
        sign, gain = signs[:, degrees - depth :], gains[:, degrees - depth :]
        held = []
        for r in range(TILE):
            starts = [h * 128 + 2 * r + p for h in range(2) for p in range(2)]
            modes = [pick(x_all, half, start, TILE, 2 * TILE) for start in starts]
            both = dot(
                jnp.concatenate(modes, axis=0).astype(BF16), table_ref[:, at + r * depth : at + (r + 1) * depth]
            )
            spectrum = both[: 2 * TILE] + sign * both[2 * TILE :]
            filtered = spectrum * gain
            held.append(jnp.concatenate([filtered, sign * filtered], axis=0).astype(BF16))
        for r in range(TILE):
            waves = dot(held[r], table_ref[:, at + r * depth : at + (r + 1) * depth], ((1,), (1,)))
            for h in range(2):
                for p in range(2):
                    i = 2 * h + p
                    place(out_all, waves[i * TILE : (i + 1) * TILE], h * 128 + 2 * r + p, TILE, 2 * TILE)
        at += TILE * depth
        for h, order in enumerate((north, south)):
            waves = pick(out_all, half, h * 128, 128).T.astype(BF16)
            for n, t in enumerate(order):
                for i in range(blocks):
                    lane = i * stride + g * 128
                    row = (n * blocks + i) * TILE
                    out_ref[t, :, lane : lane + 128] = waves[row : row + TILE]


def inverse_kernel(rows, cols, doubled, scaled, *refs):
    if scaled:
        x_ref, table_ref, scale_ref, piece_ref, out_ref, x_all = refs
    else:
        x_ref, table_ref, out_ref, x_all = refs
    bands = x_ref.shape[0]
    blocks = rows // TILE
    stride = x_ref.shape[2] // blocks
    share = 2 * TILE
    held = [
        [
            jnp.concatenate(
                [
                    x_ref[t, :, i * stride + g * 128 : i * stride + (g + 1) * 128].astype(F32)
                    for i in range(blocks)
                ],
                axis=0,
            )
            for g in range(stride // 128)
        ]
        for t in range(bands)
    ]
    for c in range(TILE):
        line = jnp.concatenate(
            [tile[:, c * share : (c + 1) * share] for one in held for tile in one], axis=1
        )
        place(x_all, line, c, rows, TILE)
    modes = table_ref.shape[0]
    x = pick(x_all, modes)
    if doubled:
        column = lax.broadcasted_iota(jnp.int32, x.shape, 1)
        x = x * jnp.where(column < 2, 1.0, 2.0)
    value = dot(x.astype(BF16), table_ref[...])
    chunks, _, lanes = out_ref.shape
    pad = lanes - rows * cols
    rest = jnp.zeros((TILE, pad), F32)
    if scaled:
        value = value * scale_ref[...]
        piece = piece_ref[...]
        rest = jnp.concatenate(
            [piece[i // 2 : i // 2 + 1, i % 2 * 64 : i % 2 * 64 + 64] for i in range(TILE)], axis=0
        )
    lines = [value[s * TILE : (s + 1) * TILE] for s in range(rows)]
    for b in range(chunks):
        parts = [line[:, b * cols : (b + 1) * cols] for line in lines]
        out_ref[b] = jnp.concatenate(parts + [rest], axis=1).astype(BF16)


def mlp_kernel(
    grad_scale,
    recv_ref, state_ref, cot_ref, up_ref, down_ref,
    send_ref, back_out,
    mixed, cots, active_all, back_pre_all, grads, back_ref, sem,
):
    rows, cols, channels = state_ref.shape
    chunks = recv_ref.shape[0]
    points = rows * cols
    mixed[...] = take_tile(recv_ref, points)
    for s in range(rows):
        at = pl.ds(s * cols, cols)
        row = slot_row(s, rows)
        mixed[at, :] = mixed[at, :] + state_ref[row].astype(F32)
        cots[at, :] = cot_ref[row].astype(F32)

    up = up_ref[...]
    mixed_low = mixed[...].astype(BF16)
    cot_low = cots[...].astype(BF16)
    pre = dot(mixed_low, up)
    back_active = dot(cot_low, down_ref[...])
    cdf = 0.5 * (1.0 + lax.erf(pre * (1.0 / math.sqrt(2.0))))
    density = jnp.exp(-0.5 * pre * pre) * (1.0 / math.sqrt(2.0 * math.pi))
    active_all[...] = (pre * cdf).astype(BF16)
    back_pre_all[...] = (back_active * (cdf + pre * density)).astype(BF16)
    back_ref[...] = cots[...] + dot(back_pre_all[...], up, ((1,), (1,)))
    kept = pltpu.make_async_copy(back_ref, back_out, sem)
    kept.start()
    up_part = dot(mixed_low, back_pre_all[...], ((0,), (0,)))
    down_part = dot(cot_low, active_all[...], ((0,), (0,)))
    place(grads, up_part * grad_scale, lead=(0,))
    place(grads, down_part * grad_scale, lead=(1,))

    used = padded(points)
    per_band = chunks // 2
    bands = channels // per_band
    hidden = up_ref.shape[1]
    for b in range(chunks):
        line = pick(grads, hidden, b // 2, bands, per_band, lead=(b % 2,)).astype(BF16)
        for i in range(bands // TILE):
            send_ref[b, :, used + i * hidden : used + (i + 1) * hidden] = line[
                i * TILE : (i + 1) * TILE
            ]
    send_tile(send_ref, back_ref[...], used)
    kept.wait()


def join_kernel(recv_ref, back_ref, out_ref, up_ref, down_ref, held):
    rows, cols, _ = out_ref.shape
    points = rows * cols
    total = back_ref[...] + take_tile(recv_ref, points)
    for s in range(rows):
        out_ref[slot_row(s, rows)] = total[s * cols : (s + 1) * cols].astype(BF16)
    lines, hidden = up_ref.shape
    share = hidden // TILE
    for b in range(recv_ref.shape[0]):
        held[pl.ds(b * TILE, TILE), :] = jnp.concatenate(
            [recv_ref[b, :, points : points + share].astype(F32), jnp.zeros((TILE, 128 - share), F32)],
            axis=1,
        )
    for parity, ref in enumerate((up_ref, down_ref)):
        ref[...] = jnp.concatenate(
            [
                held[pl.ds(parity * TILE + i, lines, stride=2 * TILE), :][:, :share]
                for i in range(TILE)
            ],
            axis=1,
        )


def body(state_grid, spectral_filter, up_weight, down_weight, cotangent):
    _, rows, cols, channels = state_grid.shape
    bands, chunks = lax.axis_size("lat"), lax.axis_size("lon")
    band = lax.axis_index("lat")
    degrees = spectral_filter.shape[0]
    hidden = up_weight.shape[1]
    lat_total, lon_total = rows * bands, cols * chunks
    orders = degrees // bands
    points = rows * cols
    used = padded(points)
    modes = 2 * degrees
    line = TILE * 2 * orders
    wide = rows // TILE * line
    tiles = orders // TILE

    state = state_grid.reshape(rows, cols, channels)
    cot = cotangent.reshape(rows, cols, channels)

    sent = call(
        split_kernel,
        shaped((chunks, TILE, used), BF16),
        state,
        scratch=[pltpu.VMEM((points, channels), F32)],
    )
    whole = lax.all_to_all(sent, "lon", 0, 0, tiled=True)

    table, turned = fourier_tables(lon_total, bands, orders)
    legendre = legendre_tables(bands, orders, lat_total, degrees)
    gains = spectral_filter.T
    own = lax.dynamic_slice_in_dim(row_scale(lat_total, lon_total), band * rows, rows)
    own = jnp.where(band * 2 >= bands, jnp.flip(own), own)
    scale = jnp.repeat(own, TILE)[:, None]

    def forward(x, doubled, skip, *extra):
        return call(
            functools.partial(forward_kernel, rows, cols, doubled, bool(extra), skip),
            shaped((bands, TILE, wide + (128 if skip else 0)), BF16),
            x, table, *extra,
            scratch=[
                pltpu.VMEM((rows * TILE, lon_total), F32),
                tiles_of(rows * TILE, modes),
            ],
        )

    def turn(x):
        return lax.all_to_all(x, "lat", 0, 0, tiled=True)

    def spectral(x, has_piece):
        outs = [shaped((bands, TILE, wide), BF16)]
        if has_piece:
            outs.append(shaped((TILE, 128), F32))
        return call(
            functools.partial(spectral_kernel, rows, tiles, has_piece),
            outs,
            x, gains, legendre,
            scratch=[tiles_of(256, lat_total // 2)] * 2,
        )

    def inverse(x, doubled, *extra):
        return call(
            functools.partial(inverse_kernel, rows, cols, doubled, bool(extra)),
            shaped((chunks, TILE, used), BF16),
            x, turned, *extra,
            scratch=[tiles_of(rows * TILE, modes)],
        )

    spread = turn(forward(whole, False, 0, scale))
    waves = turn(spectral(spread, False)[0])
    smooth = lax.all_to_all(inverse(waves, True), "lon", 0, 0, tiled=True)

    sent, back_mixed = call(
        functools.partial(mlp_kernel, 1.0 / math.sqrt(lat_total * lon_total)),
        [
            shaped((chunks, TILE, used + bands // TILE * hidden), BF16),
            shaped((points, channels), F32),
        ],
        smooth, state, cot, up_weight, down_weight,
        in_hbm=(1,),
        scratch=[
            pltpu.VMEM((points, channels), F32),
            pltpu.VMEM((points, channels), F32),
            pltpu.VMEM((points, hidden), BF16),
            pltpu.VMEM((points, hidden), BF16),
            pltpu.VMEM((2, hidden // 128, channels, 128), F32),
            pltpu.VMEM((points, channels), F32),
            pltpu.SemaphoreType.DMA,
        ],
    )
    whole = lax.all_to_all(sent, "lon", 0, 0, tiled=True)
    filtered, piece = spectral(turn(forward(whole, True, hidden)), True)
    back_waves = turn(filtered)
    field = lax.all_to_all(inverse(back_waves, False, scale, piece), "lon", 0, 0, tiled=True)
    grad_field, grad_up, grad_down = call(
        join_kernel,
        [
            shaped((rows, cols, channels), BF16),
            shaped((chunks // 2, hidden), F32),
            shaped((chunks // 2, hidden), F32),
        ],
        field, back_mixed,
        scratch=[pltpu.VMEM((chunks * TILE, 128), F32)],
    )
    return grad_field.reshape(state_grid.shape), grad_up, grad_down


def solution(mesh):
    placed = (P(None, "lat", "lon", None), P(None, "lon"), P(), P(), P(None, "lat", "lon", None))
    return jax.shard_map(
        body,
        mesh=mesh,
        in_specs=placed,
        out_specs=(P(None, "lat", "lon", None), P("lat", None), P("lat", None)),
        check_vma=False,
    )
```

```python
import functools
import math

import jax
import jax.numpy as jnp
from jax import lax
from jax.experimental import pallas as pl
from jax.experimental.pallas import tpu as pltpu
from jax.sharding import PartitionSpec as P

TILE = 8
F32 = jnp.float32
BF16 = jnp.bfloat16
VMEM_LIMIT = 24 * 1024 * 1024


def dot(a, b, dims=((1,), (0,))):
    return lax.dot_general(a, b, (dims, ((), ())), preferred_element_type=F32)


def call(kernel, outs, *args, scratch=(), cost=None, in_hbm=()):
    single = not isinstance(outs, (list, tuple))
    shapes = [outs] if single else list(outs)
    result = pl.pallas_call(
        kernel,
        out_shape=shapes,
        in_specs=[pl.BlockSpec(memory_space=pltpu.VMEM)] * len(args),
        out_specs=[
            pl.BlockSpec(memory_space=pltpu.HBM if i in in_hbm else pltpu.VMEM)
            for i in range(len(shapes))
        ],
        scratch_shapes=list(scratch),
        compiler_params=pltpu.CompilerParams(vmem_limit_bytes=VMEM_LIMIT),
        cost_estimate=cost,
    )(*args)
    return result[0] if single else result


def shaped(shape, dtype):
    return jax.ShapeDtypeStruct(shape, dtype)


def tiles_of(rows, width):
    return pltpu.VMEM((-(-width // 128), rows, 128), F32)


def pick(ref, width, start=0, size=None, stride=1, lead=()):
    tiles = -(-width // 128)
    at = slice(None) if size is None else pl.ds(start, size, stride=stride)
    value = jnp.concatenate([ref[(*lead, i, at, slice(None))] for i in range(tiles)], axis=1)
    return value[:, :width] if tiles * 128 > width else value


def place(ref, value, start=0, size=None, stride=1, lead=()):
    pad = -value.shape[1] % 128
    if pad:
        value = jnp.concatenate([value, jnp.zeros((value.shape[0], pad), value.dtype)], axis=1)
    at = slice(None) if size is None else pl.ds(start, size, stride=stride)
    for i in range(value.shape[1] // 128):
        ref[(*lead, i, at, slice(None))] = value[:, i * 128 : (i + 1) * 128]


def row_scale(lat_total, lon_total):
    colatitude = (jnp.arange(lat_total, dtype=F32) + 0.5) * (math.pi / lat_total)
    counter = jnp.arange(1, lat_total // 2 + 1, dtype=F32)
    series = jnp.sum(
        jnp.cos(2.0 * counter[None, :] * colatitude[:, None])
        / (4.0 * counter * counter - 1.0)[None, :],
        axis=1,
    )
    return 2.0 / lat_total * (1.0 - 2.0 * series) * (2.0 * math.pi / lon_total)


def wave_pair(product, lon_total):
    quarter = lon_total // 4
    turns = jnp.floor(product * (1.0 / quarter) + 0.5)
    angle = (product - turns * quarter) * (2.0 * math.pi / lon_total)
    square = angle * angle
    sine = angle * (
        1.0 + square * (-1.0 / 6 + square * (1.0 / 120 + square * (-1.0 / 5040 + square / 362880)))
    )
    cosine = 1.0 + square * (
        -0.5 + square * (1.0 / 24 + square * (-1.0 / 720 + square / 40320))
    )
    quadrant = turns - 4.0 * jnp.floor(turns * 0.25)
    odd = (quadrant == 1.0) | (quadrant == 3.0)
    first = jnp.where(odd, sine, cosine)
    second = jnp.where(odd, cosine, sine)
    first = jnp.where((quadrant == 1.0) | (quadrant == 2.0), -first, first)
    second = jnp.where(quadrant >= 2.0, -second, second)
    return first, second


def rotate(pair, turn):
    cosine, sine = pair
    turn_cos, turn_sin = turn
    return cosine * turn_cos - sine * turn_sin, sine * turn_cos + cosine * turn_sin


def phased(product, part, lon_total):
    cosine, sine = wave_pair(product, lon_total)
    return jnp.where(part == 1, -sine, cosine), jnp.where(part == 1, cosine, sine)


def fourier_kernel(bands, orders, table_out, turned_out, table_ref, turned_ref, sems):
    lon_total, modes = table_ref.shape
    per = 2 * orders

    shape = (TILE, modes)
    column = lax.broadcasted_iota(jnp.int32, shape, 1)
    group = column // per
    rank = column - group * per
    order = (bands * (rank // 2) + group).astype(F32)
    row = lax.broadcasted_iota(jnp.int32, shape, 0).astype(F32)
    turn = wave_pair(TILE * order, lon_total)

    def step(index, pair):
        later = rotate(pair, turn)
        at = pl.ds(pl.multiple_of(index * 2 * TILE, 2 * TILE), 2 * TILE)
        table_ref[at, :] = jnp.concatenate([pair[0], later[0]], axis=0).astype(BF16)
        return rotate(later, turn)

    lax.fori_loop(0, lon_total // (2 * TILE), step, phased(row * order, rank % 2, lon_total))
    first = pltpu.make_async_copy(table_ref, table_out, sems.at[0])
    first.start()

    shape = (TILE, lon_total)
    lon_index = lax.broadcasted_iota(jnp.int32, shape, 1).astype(F32)
    row = lax.broadcasted_iota(jnp.int32, shape, 0)
    start = phased((bands * (row // 2)).astype(F32) * lon_index, row % 2, lon_total)
    inner = wave_pair(TILE // 2 * bands * lon_index, lon_total)
    outer = wave_pair(lon_index, lon_total)

    def group_step(t, pair):
        now = pair
        for i in range(per // (2 * TILE)):
            later = rotate(now, inner)
            at = pl.ds(pl.multiple_of(t * per + i * 2 * TILE, 2 * TILE), 2 * TILE)
            turned_ref[at, :] = jnp.concatenate([now[0], later[0]], axis=0).astype(BF16)
            now = rotate(later, inner)
        return rotate(pair, outer)

    lax.fori_loop(0, modes // per, group_step, start)
    second = pltpu.make_async_copy(turned_ref, turned_out, sems.at[1])
    second.start()
    first.wait()
    second.wait()


def fourier_tables(lon_total, bands, orders):
    modes = 2 * bands * orders
    shapes = [(lon_total, modes), (modes, lon_total)]
    return call(
        functools.partial(fourier_kernel, bands, orders),
        [shaped(shape, BF16) for shape in shapes],
        scratch=[pltpu.VMEM(shape, BF16) for shape in shapes] + [pltpu.SemaphoreType.DMA((2,))],
        cost=pl.CostEstimate(
            flops=30 * modes * lon_total, bytes_accessed=8 * modes * lon_total, transcendentals=0
        ),
        in_hbm=(0, 1),
    )


def legendre_kernel(bands, degrees, cos_ref, diag_ref, out_ref, *tables):
    tiles = diag_ref.shape[0] // TILE
    band = lax.axis_index("lat")
    cosine = cos_ref[...]
    width = cosine.shape[1]
    shape = (TILE, 128)
    rank = lax.broadcasted_iota(jnp.int32, shape, 0)
    orders = [(bands * (TILE * g + rank) + band).astype(F32) for g in range(tiles)]
    diags = [diag_ref[g * TILE : (g + 1) * TILE, :] for g in range(tiles)]

    def spread(value):
        return jnp.concatenate([value] * (-(-width // 128)), axis=1)[:, :width]

    def block(active, index, carry):
        carry = list(carry)
        for g in range(active):
            here, before, scale, inverse = carry[g]
            order = orders[g]
            square = order * order
            wide_order = spread(order)
            level = jnp.exp(diags[g] + scale)
            for inner in range(TILE):
                degree = index * TILE + inner
                lv = jnp.full(shape, degree, jnp.int32).astype(F32)
                now = jnp.sqrt(jnp.maximum(lv * lv - square, 0.0) / jnp.maximum(4.0 * lv * lv - 1.0, 1.0))
                live = lv > order
                growth = 1.0 / jnp.where(live, now, 1.0)
                ahead = spread(growth) * cosine * here - spread(growth * inverse) * before
                wide_live = spread(lv) > wide_order
                here, before = jnp.where(wide_live, ahead, here), jnp.where(wide_live, here, before)
                values = jnp.where(spread(lv) >= wide_order, level * here, 0.0)
                at = pl.multiple_of((degree - bands * TILE * g) * TILE, TILE)
                place(tables[g], values, at, TILE)
                inverse = now
            largest = jnp.maximum(jnp.abs(here), jnp.abs(before))
            carry[g] = (here / largest, before / largest, scale + jnp.log(largest), inverse)
        return tuple(carry)

    ones = jnp.ones((TILE, width), F32)
    zeros = jnp.zeros((TILE, width), F32)
    carry = tuple((ones, zeros, zeros, jnp.zeros(shape, F32)) for _ in range(tiles))
    for g in range(tiles):
        last = bands * (g + 1) if g + 1 < tiles else degrees // TILE
        carry = lax.fori_loop(bands * g, last, functools.partial(block, g + 1), carry)
    at = 0
    for g in range(tiles):
        depth = degrees - bands * TILE * g
        for r in range(TILE):
            rows = pick(tables[g], width, r, depth, TILE)
            out_ref[:, at : at + depth] = rows.T.astype(BF16)
            at += depth


def legendre_tables(bands, orders, lat_total, degrees):
    half = lat_total // 2
    colatitude = (jnp.arange(half, dtype=F32) + 0.5) * (math.pi / lat_total)
    cosine = jnp.cos(colatitude)
    log_sine = jnp.log(jnp.sin(colatitude))
    later = jnp.arange(1, degrees, dtype=F32)
    ratios = jnp.log((2.0 * later - 1.0) / (2.0 * later))
    order = (bands * jnp.arange(orders, dtype=jnp.int32) + lax.axis_index("lat")).astype(F32)
    partial_logs = jnp.sum(jnp.where(later[None, :] <= order[:, None], ratios[None, :], 0.0), axis=1)
    base_logs = 0.5 * (jnp.log((2.0 * order + 1.0) / (4.0 * math.pi)) + partial_logs)
    diag = base_logs[:, None] + order[:, None] * log_sine[None, :]
    depths = [degrees - bands * TILE * g for g in range(orders // TILE)]
    return call(
        functools.partial(legendre_kernel, bands, degrees),
        shaped((half, TILE * sum(depths)), BF16),
        jnp.broadcast_to(cosine[None, :], (TILE, half)),
        diag,
        scratch=[tiles_of(depth * TILE, half) for depth in depths],
        cost=pl.CostEstimate(flops=40_000_000, bytes_accessed=6_000_000, transcendentals=1_000_000),
    )


def slot_row(slot, rows):
    south = lax.axis_index("lat") * 2 >= lax.axis_size("lat")
    return jnp.where(south, rows - 1 - slot, slot)


def padded(count):
    return -(-count // 128) * 128


def send_tile(ref, grid, used):
    turned = grid.T
    pad = used - turned.shape[1]
    if pad:
        turned = jnp.concatenate([turned, jnp.zeros((turned.shape[0], pad), F32)], axis=1)
    for b in range(ref.shape[0]):
        ref[b, :, :used] = turned[b * TILE : (b + 1) * TILE].astype(BF16)


def take_tile(ref, points):
    chunks = [ref[b].astype(F32) for b in range(ref.shape[0])]
    return jnp.concatenate(chunks, axis=0).T[:points]


def split_kernel(x_ref, out_ref, grid):
    rows, cols, _ = x_ref.shape
    for s in range(rows):
        grid[pl.ds(s * cols, cols), :] = x_ref[slot_row(s, rows)].astype(F32)
    send_tile(out_ref, grid[...], out_ref.shape[2])


def forward_kernel(rows, cols, doubled, scaled, skip, *refs):
    if scaled:
        x_ref, table_ref, scale_ref, out_ref, x_all, out_all = refs
    else:
        x_ref, table_ref, out_ref, x_all, out_all = refs
    chunks = x_ref.shape[0]
    used = padded(rows * cols)
    held = [x_ref[b, :, :used].astype(F32) for b in range(chunks)]
    for s in range(rows):
        x_all[pl.ds(s * TILE, TILE), :] = jnp.concatenate(
            [one[:, s * cols : (s + 1) * cols] for one in held], axis=1
        )
    value = dot(x_all[...].astype(BF16), table_ref[...])
    if scaled:
        value = value * scale_ref[...]
    if doubled:
        column = lax.broadcasted_iota(jnp.int32, value.shape, 1)
        value = value * jnp.where(column < 2, 1.0, 2.0)
    modes = value.shape[1]
    place(out_all, value)
    lines = [pick(out_all, modes, c, rows, TILE) for c in range(TILE)]
    bands = out_ref.shape[0]
    per = modes // bands
    line_lanes = TILE * per
    for t in range(bands):
        tile = jnp.concatenate([line[:, t * per : (t + 1) * per] for line in lines], axis=1)
        tile = tile.astype(BF16)
        for i in range(rows // TILE):
            out_ref[t, :, i * line_lanes : (i + 1) * line_lanes] = tile[i * TILE : (i + 1) * TILE]
    if skip:
        total = x_ref[0, :, used:].astype(F32)
        for b in range(1, chunks):
            total = total + x_ref[b, :, used:].astype(F32)
        lane = TILE * per * (rows // TILE)
        for t in range(bands):
            at = t // TILE * skip
            parts = [
                total[t % TILE : t % TILE + 1, at + i * 128 : at + (i + 1) * 128]
                for i in range(skip // 128)
            ]
            parts.append(jnp.zeros((TILE - skip // 128, 128), F32))
            out_ref[t, :, lane : lane + 128] = jnp.concatenate(parts, axis=0).astype(BF16)


def spectral_kernel(rows, tiles, has_piece, x_ref, filter_ref, table_ref, out_ref, *refs):
    x_all, out_all = refs[-2:]
    bands = x_ref.shape[0]
    blocks = rows // TILE
    stride = tiles * 128
    degrees = filter_ref.shape[1]
    half = table_ref.shape[0]
    if has_piece:
        total = x_ref[0, :, blocks * stride :].astype(F32)
        for t in range(1, bands):
            total = total + x_ref[t, :, blocks * stride :].astype(F32)
        refs[0][...] = total
    shape = (2 * TILE, degrees)
    odd = (lax.broadcasted_iota(jnp.int32, shape, 1) + lax.axis_index("lat")) % 2
    signs = (1 - 2 * odd).astype(F32)
    gains = jnp.concatenate([filter_ref[...], filter_ref[...]], axis=0)
    north = list(range(bands // 2))
    south = [bands - 1 - t for t in north]
    for h, order in enumerate((north, south)):
        for g in range(tiles):
            parts = [
                x_ref[t, :, i * stride + g * 128 : i * stride + (g + 1) * 128].astype(F32)
                for t in order
                for i in range(blocks)
            ]
            place(x_all, jnp.concatenate(parts, axis=0).T, h * stride + g * 128, 128)
    step = stride // TILE
    at = 0
    for g in range(tiles):
        depth = degrees - bands * TILE * g
        sign, gain = signs[:, degrees - depth :], gains[:, degrees - depth :]
        held = []
        for r in range(TILE):
            starts = [h * stride + 2 * (g * TILE + r) + p for h in range(2) for p in range(2)]
            modes = [pick(x_all, half, start, TILE, step) for start in starts]
            table = table_ref[:, at : at + depth]
            both = dot(jnp.concatenate(modes, axis=0).astype(BF16), table)
            filtered = (both[: 2 * TILE] + sign * both[2 * TILE :]) * gain
            filtered = jnp.concatenate([filtered, sign * filtered], axis=0).astype(BF16)
            held.append((at, starts, filtered))
            at += depth
        for first, starts, filtered in held:
            waves = dot(filtered, table_ref[:, first : first + depth], ((1,), (1,)))
            for i, start in enumerate(starts):
                place(out_all, waves[i * TILE : (i + 1) * TILE], start, TILE, step)
    for h, order in enumerate((north, south)):
        for g in range(tiles):
            waves = pick(out_all, half, h * stride + g * 128, 128).T.astype(BF16)
            for n, t in enumerate(order):
                for i in range(blocks):
                    lane = i * stride + g * 128
                    row = (n * blocks + i) * TILE
                    out_ref[t, :, lane : lane + 128] = waves[row : row + TILE]


def inverse_kernel(rows, cols, doubled, scaled, *refs):
    if scaled:
        x_ref, table_ref, scale_ref, piece_ref, out_ref, x_all = refs
    else:
        x_ref, table_ref, out_ref, x_all = refs
    bands = x_ref.shape[0]
    blocks = rows // TILE
    stride = x_ref.shape[2] // blocks
    share = stride // TILE
    held = [
        jnp.concatenate(
            [x_ref[t, :, i * stride : (i + 1) * stride].astype(F32) for i in range(blocks)], axis=0
        )
        for t in range(bands)
    ]
    for c in range(TILE):
        line = jnp.concatenate([one[:, c * share : (c + 1) * share] for one in held], axis=1)
        place(x_all, line, c, rows, TILE)
    modes = table_ref.shape[0]
    x = pick(x_all, modes)
    if doubled:
        column = lax.broadcasted_iota(jnp.int32, x.shape, 1)
        x = x * jnp.where(column < 2, 1.0, 2.0)
    value = dot(x.astype(BF16), table_ref[...])
    chunks, _, lanes = out_ref.shape
    pad = lanes - rows * cols
    rest = jnp.zeros((TILE, pad), F32)
    if scaled:
        value = value * scale_ref[...]
        piece = piece_ref[...]
        rest = jnp.concatenate(
            [piece[i // 2 : i // 2 + 1, i % 2 * 64 : i % 2 * 64 + 64] for i in range(TILE)], axis=0
        )
    lines = [value[s * TILE : (s + 1) * TILE] for s in range(rows)]
    for b in range(chunks):
        parts = [line[:, b * cols : (b + 1) * cols] for line in lines]
        out_ref[b] = jnp.concatenate(parts + [rest], axis=1).astype(BF16)


def mlp_kernel(
    grad_scale,
    recv_ref, state_ref, cot_ref, up_ref, down_ref,
    send_ref, back_out,
    mixed, cots, active_all, back_pre_all, grads, back_ref, sem,
):
    rows, cols, channels = state_ref.shape
    chunks = recv_ref.shape[0]
    points = rows * cols
    mixed[...] = take_tile(recv_ref, points)
    for s in range(rows):
        at = pl.ds(s * cols, cols)
        row = slot_row(s, rows)
        mixed[at, :] = mixed[at, :] + state_ref[row].astype(F32)
        cots[at, :] = cot_ref[row].astype(F32)

    up = up_ref[...]
    mixed_low = mixed[...].astype(BF16)
    cot_low = cots[...].astype(BF16)
    pre = dot(mixed_low, up)
    back_active = dot(cot_low, down_ref[...])
    cdf = 0.5 * (1.0 + lax.erf(pre * (1.0 / math.sqrt(2.0))))
    density = jnp.exp(-0.5 * pre * pre) * (1.0 / math.sqrt(2.0 * math.pi))
    active_all[...] = (pre * cdf).astype(BF16)
    back_pre_all[...] = (back_active * (cdf + pre * density)).astype(BF16)
    back_ref[...] = cots[...] + dot(back_pre_all[...], up, ((1,), (1,)))
    kept = pltpu.make_async_copy(back_ref, back_out, sem)
    kept.start()
    up_part = dot(mixed_low, back_pre_all[...], ((0,), (0,)))
    down_part = dot(cot_low, active_all[...], ((0,), (0,)))
    place(grads, up_part * grad_scale, lead=(0,))
    place(grads, down_part * grad_scale, lead=(1,))

    used = padded(points)
    per_band = chunks // 2
    bands = channels // per_band
    hidden = up_ref.shape[1]
    for b in range(chunks):
        line = pick(grads, hidden, b // 2, bands, per_band, lead=(b % 2,)).astype(BF16)
        for i in range(bands // TILE):
            send_ref[b, :, used + i * hidden : used + (i + 1) * hidden] = line[
                i * TILE : (i + 1) * TILE
            ]
    send_tile(send_ref, back_ref[...], used)
    kept.wait()


def join_kernel(recv_ref, back_ref, out_ref, up_ref, down_ref, held):
    rows, cols, _ = out_ref.shape
    points = rows * cols
    total = back_ref[...] + take_tile(recv_ref, points)
    for s in range(rows):
        out_ref[slot_row(s, rows)] = total[s * cols : (s + 1) * cols].astype(BF16)
    lines, hidden = up_ref.shape
    share = hidden // TILE
    for b in range(recv_ref.shape[0]):
        held[pl.ds(b * TILE, TILE), :] = jnp.concatenate(
            [recv_ref[b, :, points : points + share].astype(F32), jnp.zeros((TILE, 128 - share), F32)],
            axis=1,
        )
    for parity, ref in enumerate((up_ref, down_ref)):
        ref[...] = jnp.concatenate(
            [
                held[pl.ds(parity * TILE + i, lines, stride=2 * TILE), :][:, :share]
                for i in range(TILE)
            ],
            axis=1,
        )


def body(state_grid, spectral_filter, up_weight, down_weight, cotangent):
    _, rows, cols, channels = state_grid.shape
    bands, chunks = lax.axis_size("lat"), lax.axis_size("lon")
    band = lax.axis_index("lat")
    degrees = spectral_filter.shape[0]
    hidden = up_weight.shape[1]
    lat_total, lon_total = rows * bands, cols * chunks
    orders = degrees // bands
    points = rows * cols
    used = padded(points)
    modes = 2 * degrees
    line = TILE * 2 * orders
    wide = rows // TILE * line
    tiles = orders // TILE

    state = state_grid.reshape(rows, cols, channels)
    cot = cotangent.reshape(rows, cols, channels)

    sent = call(
        split_kernel,
        shaped((chunks, TILE, used), BF16),
        state,
        scratch=[pltpu.VMEM((points, channels), F32)],
    )
    whole = lax.all_to_all(sent, "lon", 0, 0, tiled=True)

    table, turned = fourier_tables(lon_total, bands, orders)
    legendre = legendre_tables(bands, orders, lat_total, degrees)
    gains = spectral_filter.T
    own = lax.dynamic_slice_in_dim(row_scale(lat_total, lon_total), band * rows, rows)
    own = jnp.where(band * 2 >= bands, jnp.flip(own), own)
    scale = jnp.repeat(own, TILE)[:, None]

    def forward(x, doubled, skip, *extra):
        return call(
            functools.partial(forward_kernel, rows, cols, doubled, bool(extra), skip),
            shaped((bands, TILE, wide + (128 if skip else 0)), BF16),
            x, table, *extra,
            scratch=[
                pltpu.VMEM((rows * TILE, lon_total), F32),
                tiles_of(rows * TILE, modes),
            ],
        )

    def turn(x):
        return lax.all_to_all(x, "lat", 0, 0, tiled=True)

    def spectral(x, has_piece):
        outs = [shaped((bands, TILE, wide), BF16)]
        if has_piece:
            outs.append(shaped((TILE, 128), F32))
        return call(
            functools.partial(spectral_kernel, rows, tiles, has_piece),
            outs,
            x, gains, legendre,
            scratch=[tiles_of(2 * line, lat_total // 2)] * 2,
        )

    def inverse(x, doubled, *extra):
        return call(
            functools.partial(inverse_kernel, rows, cols, doubled, bool(extra)),
            shaped((chunks, TILE, used), BF16),
            x, turned, *extra,
            scratch=[tiles_of(rows * TILE, modes)],
        )

    spread = turn(forward(whole, False, 0, scale))
    waves = turn(spectral(spread, False)[0])
    smooth = lax.all_to_all(inverse(waves, True), "lon", 0, 0, tiled=True)

    sent, back_mixed = call(
        functools.partial(mlp_kernel, 1.0 / math.sqrt(lat_total * lon_total)),
        [
            shaped((chunks, TILE, used + bands // TILE * hidden), BF16),
            shaped((points, channels), F32),
        ],
        smooth, state, cot, up_weight, down_weight,
        in_hbm=(1,),
        scratch=[
            pltpu.VMEM((points, channels), F32),
            pltpu.VMEM((points, channels), F32),
            pltpu.VMEM((points, hidden), BF16),
            pltpu.VMEM((points, hidden), BF16),
            pltpu.VMEM((2, hidden // 128, channels, 128), F32),
            pltpu.VMEM((points, channels), F32),
            pltpu.SemaphoreType.DMA,
        ],
    )
    whole = lax.all_to_all(sent, "lon", 0, 0, tiled=True)
    filtered, piece = spectral(turn(forward(whole, True, hidden)), True)
    back_waves = turn(filtered)
    field = lax.all_to_all(inverse(back_waves, False, scale, piece), "lon", 0, 0, tiled=True)
    grad_field, grad_up, grad_down = call(
        join_kernel,
        [
            shaped((rows, cols, channels), BF16),
            shaped((chunks // 2, hidden), F32),
            shaped((chunks // 2, hidden), F32),
        ],
        field, back_mixed,
        scratch=[pltpu.VMEM((chunks * TILE, 128), F32)],
    )
    return grad_field.reshape(state_grid.shape), grad_up, grad_down


def solution(mesh):
    placed = (P(None, "lat", "lon", None), P(None, "lon"), P(), P(), P(None, "lat", "lon", None))
    return jax.shard_map(
        body,
        mesh=mesh,
        in_specs=placed,
        out_specs=(P(None, "lat", "lon", None), P("lat", None), P("lat", None)),
        check_vma=False,
    )
```
